256 devices in a mesh: role: 2 (over x_hi), ctx: 16 (over z, core), tp: 8 (over x_lo, y).
Axes of the slice: x: 4 (x_hi: 2, x_lo: 2; x = x_hi * 2 + x_lo), y: 4, z: 8, core: 2. Of those that a mesh axis runs over, the one named last changes fastest.
Arguments:
- prefill_query: bfloat16 [2, 1024, 12288], P('role', 'ctx', 'tp'), may hold values from -130 to 130
- prefix_kv: bfloat16 [2, 2, 4096, 1024], P('role', None, 'ctx', 'tp'), may hold values from -6 to 6
- new_kv: bfloat16 [2, 2, 1024, 1024], P('role', None, 'ctx', 'tp'), may hold values from -6 to 6
- new_exponent: int32 [2, 2, 64, 8], P('role', None, 'ctx', 'tp'), may hold values from -3 to 2
- block_shift: int32 [2, 4], replicated, may hold values from 0 to 15, as said below
- decode_query: bfloat16 [2, 32, 12288], P('role', 'ctx', 'tp'), may hold values from -200 to 200
- decode_cache: bfloat16 [2, 2, 32, 2048, 1024], P('role', None, 'ctx', None, 'tp'), may hold values from -6 to 6
- cache_exponent: int32 [2, 2, 32, 16, 8], P('role', None, 'ctx', None, 'tp'), may hold values from -1 to 2
- cache_length: int32 [2, 32], P('role', 'ctx'), may hold values from 1 to 2048, 32768 in all within a row
- decode_new_kv: bfloat16 [2, 2, 32, 1024], P('role', None, 'ctx', 'tp'), may hold values from -6 to 6
- out_weight: bfloat16 [12288, 12288], P('tp', 'ctx'), may hold values from -0.5 to 0.5
- decode_residual: bfloat16 [2, 32, 12288], P('role', 'tp', 'ctx'), may hold values from -6 to 6
Outputs:
- prefill_attn: bfloat16 [2, 1024, 12288], P('role', 'ctx', 'tp')
- shipped: bfloat16 [2, 2, 1024, 1024], P('role', None, 'ctx', 'tp')
- decode_out: bfloat16 [2, 32, 12288], P('role', 'tp', 'ctx')
The draws below stay inside these ranges and needn't reach their ends.
Inputs may be any that keep to these rules, and one draw needn't show every extreme that they name: The 4 values of block_shift of one group are distinct; block j of every prefill shard c of group g goes to decode owner (c + block_shift[g, j]) mod 16 of the other group.
All inputs are finite; a program needn't handle non-finite values. No bound on the sum of `cache_length` on one device may be relied on, other than what follows from the above.
Results may differ from the reference program's by a relative error of at most 0.018.
Values may be sent and summed in bfloat16 or wider, within the bound.
A program may use at most 64 MiB of HBM per device.

```python
import math
import jax
import jax.numpy as jnp
import numpy as np
from jax import lax

D = 12288
HEADS = 96
KEY_VALUE_HEADS = 8
HEAD_DIM = 128
STRETCH_DEV = 64
BLOCK = 16
CACHE = 2048
CBLK = 128
PREFIX = 4096
NEW = 1024
BLOCKS_DEV = 4
DEC_ROWS = 32
N_ROLE = 2
N_CTX = 16


def shared_prefix(key):
    return jax.random.normal(key, (N_ROLE, 2, PREFIX, KEY_VALUE_HEADS * HEAD_DIM), jnp.float32)


def shared_cache(key):
    return jax.random.normal(key, (N_ROLE, 2, DEC_ROWS, CACHE, KEY_VALUE_HEADS * HEAD_DIM), jnp.float32)


def draw_prefix_kv(key, part):
    base = shared_prefix(key)
    return jnp.clip(base, -6.0, 6.0).astype(jnp.bfloat16)


def draw_prefill_query(key, part):
    key = jax.random.fold_in(key, 2)
    query = jnp.clip(jax.random.normal(key, (N_ROLE, NEW, HEADS * HEAD_DIM), jnp.float32), -6.0, 6.0)
    return query.astype(jnp.bfloat16)


def draw_decode_cache(key, part):
    base = shared_cache(key)
    return jnp.clip(base, -6.0, 6.0).astype(jnp.bfloat16)


def draw_decode_query(key, part):
    key = jax.random.fold_in(key, 4)
    query = jnp.clip(jax.random.normal(key, (N_ROLE, DEC_ROWS, HEADS * HEAD_DIM), jnp.float32), -6.0, 6.0)
    return query.astype(jnp.bfloat16)


def draw_block_shift(key, part):
    key = jax.random.fold_in(key, 5)
    subkeys = jax.random.split(key, N_ROLE)
    rows = [jax.random.permutation(subkeys[index], N_CTX)[:BLOCKS_DEV] for index in range(N_ROLE)]
    return jnp.stack(rows).astype(jnp.int32)


def with_ends(result, rng, low, high):
    spot = [jax.random.randint(jax.random.fold_in(rng, axis), (), 0, length) for axis, length in enumerate(result.shape)]
    longest = result.shape.index(max(result.shape))
    neighbour = spot[:longest] + [(spot[longest] + 1) % result.shape[longest]] + spot[longest + 1:]
    return result.at[tuple(spot)].set(low).at[tuple(neighbour)].set(high)


def level_of(rng, shape, cuts, least, top_value):
    loudness = 1.0
    for dim, blocks in cuts:
        heights = jax.random.uniform(jax.random.fold_in(jax.random.fold_in(rng, 6), dim), (blocks,), jnp.float32, least / len(cuts), top_value / len(cuts))
        loudness = loudness * jnp.repeat(jnp.exp(heights), shape[dim] // blocks).reshape((-1,) + (1,) * (len(shape) - 1 - dim))
    return loudness


def split_up(count, total, bound, lean):
    portions = [(1 << 20) // math.isqrt(rank ** lean) + 1 for rank in range(2, count + 1)]
    surplus, given = total - bound - (count - 1), [1] * (count - 1)
    while surplus > 0:
        free = [i for i in range(count - 1) if given[i] < bound]
        mass, budget = sum([portions[i] for i in free]), surplus
        for i in free:
            extra = min(bound - given[i], max(1, budget * portions[i] // mass), surplus)
            given[i] = given[i] + extra
            surplus = surplus - extra
    return np.array([bound] + given)


def ragged(own_key, count, total, bound, skew):
    if count == 2:
        one = jax.random.randint(own_key, (), max(1, total - bound), min(bound, total - 1) + 1)
        return jnp.stack([one, total - one])
    tallies = jnp.asarray(split_up(count, total, bound, skew), jnp.int32)
    pairs = (count - 1) // 2
    donor, taker = tallies[1:1 + 2 * pairs:2], tallies[2:2 + 2 * pairs:2]
    margin = jnp.minimum(donor - 1, bound - taker)
    passed = jax.random.randint(jax.random.fold_in(own_key, 1), (pairs,), 0, 1 << 20) % (margin + 1)
    tallies = tallies.at[1:1 + 2 * pairs:2].set(donor - passed).at[2:2 + 2 * pairs:2].set(taker + passed)
    return tallies[jax.random.permutation(jax.random.fold_in(own_key, 2), count)]


def noise(key, extent, spread, limit, shards=(), kind=jnp.bfloat16):
    factor_of = level_of(key, extent, shards, -0.22, 0.18) if shards else 1.0
    values = jax.random.normal(key, extent, jnp.float32) * spread * factor_of
    return jnp.minimum(jnp.maximum(values, -limit), limit).astype(kind)


def setup_inputs(seed: int = 0) -> dict:
    key_of = jax.random.split(jax.random.key(seed), 13)
    prefill_query = draw_prefill_query(jax.random.fold_in(key_of[12], 71), 0)
    prefix_kv = draw_prefix_kv(jax.random.fold_in(key_of[12], 71), 0)
    new_kv = noise(key_of[2], (N_ROLE, 2, NEW, KEY_VALUE_HEADS * HEAD_DIM), 1.0, 6.0, ((0, 2), (2, 16), (3, 8)))
    new_exponent = with_ends(jax.random.randint(key_of[3], (N_ROLE, 2, NEW // BLOCK, KEY_VALUE_HEADS), -3, 3), jax.random.fold_in(key_of[3], 1), -3, 2).astype(jnp.int32)
    block_shift = draw_block_shift(jax.random.fold_in(key_of[12], 71), 0)
    decode_query = draw_decode_query(jax.random.fold_in(key_of[12], 71), 0)
    decode_cache = draw_decode_cache(jax.random.fold_in(key_of[12], 71), 0)
    cache_exponent = with_ends(jax.random.randint(key_of[7], (N_ROLE, 2, DEC_ROWS, CACHE // CBLK, KEY_VALUE_HEADS), -1, 3), jax.random.fold_in(key_of[7], 1), -1, 2).astype(jnp.int32)
    cache_length = jax.vmap(lambda own: ragged(own, DEC_ROWS, DEC_ROWS * CACHE // 2, CACHE, 2))(jax.random.split(key_of[8], N_ROLE)).reshape((N_ROLE, DEC_ROWS)).astype(jnp.int32)
    decode_new_kv = noise(key_of[9], (N_ROLE, 2, DEC_ROWS, KEY_VALUE_HEADS * HEAD_DIM), 1.0, 6.0, ((0, 2), (2, 16), (3, 8)))
    out_weight = noise(key_of[10], (HEADS * HEAD_DIM, D), HEAD_DIM ** -0.5, 0.5, ((0, 8), (1, 16)))
    decode_residual = noise(key_of[11], (N_ROLE, DEC_ROWS, D), 1.0, 6.0, ((0, 2), (1, 8), (2, 16)))
    return {"prefill_query": prefill_query, "prefix_kv": prefix_kv, "new_kv": new_kv, "new_exponent": new_exponent, "block_shift": block_shift, "decode_query": decode_query, "decode_cache": decode_cache, "cache_exponent": cache_exponent, "cache_length": cache_length, "decode_new_kv": decode_new_kv, "out_weight": out_weight, "decode_residual": decode_residual}


def attend(query, keys, values, live):
    scores = jnp.dot(query.astype(jnp.float32), keys.astype(jnp.float32).T, precision=lax.Precision.HIGHEST, preferred_element_type=jnp.float32) * (HEAD_DIM ** -0.5)
    scores = jnp.where(live, scores, jnp.float32(-1.0e30))
    top = jnp.max(scores, axis=-1, keepdims=True)
    attention_weights = jnp.where(live, jnp.exp(scores - top), jnp.float32(0.0))
    total = jnp.sum(attention_weights, axis=-1, keepdims=True)
    rounded = attention_weights.astype(jnp.bfloat16).astype(jnp.float32)
    mixed = jnp.dot(rounded, values.astype(jnp.float32), precision=lax.Precision.HIGHEST, preferred_element_type=jnp.float32)
    return (mixed / total).astype(jnp.bfloat16)


def reference(prefill_query, prefix_kv, new_kv, new_exponent, block_shift, decode_query, decode_cache, cache_exponent, cache_length, decode_new_kv, out_weight, decode_residual):
    group_size = HEADS // KEY_VALUE_HEADS
    zero = jnp.zeros((), jnp.int32)

    def prefill_item(item):
        group = item // HEADS
        head = item % HEADS
        kv_head = head // group_size
        query = lax.dynamic_slice(prefill_query, (group, zero, head * HEAD_DIM), (1, NEW, HEAD_DIM))[0]
        older = lax.dynamic_slice(prefix_kv, (group, zero, zero, kv_head * HEAD_DIM), (1, 2, PREFIX, HEAD_DIM))[0]
        fresh = lax.dynamic_slice(new_kv, (group, zero, zero, kv_head * HEAD_DIM), (1, 2, NEW, HEAD_DIM))[0]
        keys = jnp.concatenate([older[0], fresh[0]], axis=0)
        values = jnp.concatenate([older[1], fresh[1]], axis=0)
        columns = jnp.arange(PREFIX + NEW, dtype=jnp.int32)
        tokens = jnp.arange(NEW, dtype=jnp.int32)
        live = (columns[None, :] < PREFIX) | (columns[None, :] - PREFIX <= tokens[:, None])
        return attend(query, keys, values, live)

    heads_out = lax.map(prefill_item, jnp.arange(N_ROLE * HEADS, dtype=jnp.int32))
    prefill_attn = heads_out.reshape(N_ROLE, HEADS, NEW, HEAD_DIM).transpose(0, 2, 1, 3).reshape(N_ROLE, NEW, HEADS * HEAD_DIM)

    factor = jnp.exp2(-new_exponent.astype(jnp.float32))
    cache_blocks = new_kv.astype(jnp.float32).reshape(N_ROLE, 2, NEW // BLOCK, BLOCK, KEY_VALUE_HEADS, HEAD_DIM)
    codes = (cache_blocks * factor[:, :, :, None, :, None]).astype(jnp.bfloat16).reshape(N_ROLE, 2, NEW, KEY_VALUE_HEADS * HEAD_DIM)
    rows = jnp.arange(NEW, dtype=jnp.int32)
    owner = rows // STRETCH_DEV
    slot = (rows % STRETCH_DEV) // BLOCK
    inner = rows % BLOCK
    received = []
    for group in range(N_ROLE):
        sender = N_ROLE - 1 - group
        source = (owner - block_shift[sender][slot]) % N_CTX
        source_row = (source * STRETCH_DEV + slot * BLOCK + inner).astype(jnp.int32)
        received.append(codes[sender][:, source_row])
    shipped = jnp.stack(received)

    def decode_item(item):
        group = item // (DEC_ROWS * KEY_VALUE_HEADS)
        row = (item // KEY_VALUE_HEADS) % DEC_ROWS
        kv_head = item % KEY_VALUE_HEADS
        query = lax.dynamic_slice(decode_query, (group, row, kv_head * group_size * HEAD_DIM), (1, 1, group_size * HEAD_DIM)).reshape(group_size, HEAD_DIM)
        stored = lax.dynamic_slice(decode_cache, (group, zero, row, zero, kv_head * HEAD_DIM), (1, 2, 1, CACHE, HEAD_DIM)).reshape(2, CACHE, HEAD_DIM)
        powers = lax.dynamic_slice(cache_exponent, (group, zero, row, zero, kv_head), (1, 2, 1, CACHE // CBLK, 1)).reshape(2, CACHE // CBLK)
        score_scale = jnp.repeat(jnp.exp2(powers.astype(jnp.float32)), CBLK, axis=1)
        plain = (stored.astype(jnp.float32) * score_scale[:, :, None]).astype(jnp.bfloat16)
        self_score = lax.dynamic_slice(decode_new_kv, (group, zero, row, kv_head * HEAD_DIM), (1, 2, 1, HEAD_DIM)).reshape(2, 1, HEAD_DIM)
        keys = jnp.concatenate([plain[0], self_score[0]], axis=0)
        values = jnp.concatenate([plain[1], self_score[1]], axis=0)
        length = lax.dynamic_slice(cache_length, (group, row), (1, 1))[0, 0]
        live = jnp.concatenate([jnp.arange(CACHE, dtype=jnp.int32) < length, jnp.ones((1,), dtype=bool)])
        return attend(query, keys, values, live[None, :])

    decode_heads = lax.map(decode_item, jnp.arange(N_ROLE * DEC_ROWS * KEY_VALUE_HEADS, dtype=jnp.int32))
    decode_attn = decode_heads.reshape(N_ROLE * DEC_ROWS, HEADS * HEAD_DIM)
    projected = jnp.dot(decode_attn, out_weight, preferred_element_type=jnp.float32)
    decode_out = (decode_residual.astype(jnp.float32) + projected.reshape(N_ROLE, DEC_ROWS, D)).astype(jnp.bfloat16)
    return prefill_attn, shipped, decode_out
```

```python
import jax
import jax.numpy as jnp
from jax import lax
from jax.experimental import pallas as pl
from jax.experimental.pallas import tpu as pltpu
from jax.sharding import PartitionSpec as P

MESH = pl.DeviceIdType.MESH
BF16 = jnp.bfloat16
F32 = jnp.float32
HD = 128
GROUP = 12
TOK = 64
PRE = 256
HALF = PRE // 2
ROWS = GROUP * TOK
N_CTX = 16
N_TP = 8
FAC = 16
NEWR = 2 * TOK + FAC
CACHE = 2048
CBLK = 128
DOUT = 768
LOG2E = 1.4426950408889634
SCALE2 = HD**-0.5 * LOG2E
CHUNK = 256
NEG = -1e30
NT = (((1,), (1,)), ((), ()))


def column(row):
    n = row.shape[1]
    wide = jnp.broadcast_to(row.astype(F32), (n, n))
    on = lax.broadcasted_iota(jnp.int32, (n, n), 0) == lax.broadcasted_iota(jnp.int32, (n, n), 1)
    return jnp.sum(jnp.where(on, wide, 0.0), axis=1, keepdims=True)


def kernel(
    q_hbm, prefix, new, nexp, shift_in, dq, cache, cexp, clen_in, dnew, w, resid,
    out_attn, out_ship, out_dec,
    gp, gn, nraw, ne, q_in, q_rows, m_ref, acc_ref,
    dq_in, dq_rows, cache_v, ce, dn, ga, gaf, w_v, t_out, t_in, res_v, ship_out, ship_in,
    part_o, part_s, back_o, back_s, far_v, shift, clen,
    lsem, ring_s, ring_r, q_s, q_r, at_s, at_r, tp_s, tp_r, sh_s, sh_r, po_s, po_r, ps_s, ps_r, far_s, far_r,
):
    role, p, tp = lax.axis_index("role"), lax.axis_index("ctx"), lax.axis_index("tp")
    core = lax.rem(p, 2)
    z = p // 2
    right, left = lax.rem(p + 2, N_CTX), lax.rem(p + N_CTX - 2, N_CTX)
    sib = p + 1 - 2 * core

    bar = pltpu.get_barrier_semaphore()
    for d in range(1, 8):
        pl.semaphore_signal(bar, inc=1, device_id={"ctx": lax.rem(p + 2 * d, N_CTX)}, device_id_type=MESH)
    pl.semaphore_signal(bar, inc=1, device_id={"ctx": sib}, device_id_type=MESH)
    for d in range(1, N_TP):
        pl.semaphore_signal(bar, inc=1, device_id={"tp": lax.rem(tp + d, N_TP)}, device_id_type=MESH)
    for c in (p, sib):
        pl.semaphore_signal(bar, inc=1, device_id={"role": 1 - role, "ctx": c}, device_id_type=MESH)

    loads = [
        (new.at[0], nraw), (nexp.at[0], ne), (prefix.at[0], gp.at[z]),
        (dq.at[0], dq_in), (cexp.at[0], ce), (dnew.at[0], dn),
        (cache.at[0, 0], cache_v.at[0]), (cache.at[0, 1], cache_v.at[1]),
        (q_hbm.at[0], q_in), (w, w_v), (resid.at[0], res_v), (shift_in, shift), (clen_in, clen),
    ]
    ld = [pltpu.make_async_copy(s, d, lsem.at[i]) for i, (s, d) in enumerate(loads)]
    for c in ld:
        c.start()

    pl.semaphore_wait(bar, 17)

    dev = (right, left)
    kinds = {h: ((0, 1, 2), (0, 2, 1)) for h in (1, 2, 3)}
    kinds[4] = ((3, 1), (4, 2))
    slot = {}
    for dr in (0, 1):
        for h in (1, 2, 3, 4):
            for kd in kinds[h][dr]:
                slot[(dr, h, kd)] = len(slot)

    def part(src, kd):
        if kd == 0:
            return gn.at[src]
        if kd == 1:
            return gp.at[src, :, 0:HALF]
        if kd == 2:
            return gp.at[src, :, HALF:PRE]
        if kd == 3:
            return gn.at[src, 0 : TOK + FAC]
        return gn.at[src, TOK + FAC : NEWR]

    def origin(dr, h):
        return lax.rem(z + (8 - h if dr == 0 else h), 8)

    def ring_copy(src, kd, dr, h, held=None):
        i = slot[(dr, h, kd)]
        return pltpu.make_async_remote_copy(
            src_ref=part(src, kd) if held is None else held, dst_ref=part(src, kd), send_sem=ring_s.at[i], recv_sem=ring_r.at[i],
            device_id={"ctx": dev[dr]}, device_id_type=MESH,
        )

    sends = []

    def start(c):
        c.start()
        sends.append(c)

    def post(j):
        for dr in (0, 1):
            kd = kinds[1][dr][j]
            src = gn.at[z] if j == 0 else prefix.at[0, :, 0:HALF] if kd == 1 else prefix.at[0, :, HALF:PRE]
            start(ring_copy(z, kd, dr, 1, src))

    def pump(h, j):
        for dr in (0, 1):
            kd = kinds[h][dr][j]
            src = origin(dr, h)
            ring_copy(src, kd, dr, h).wait_recv()
            if h < 3:
                start(ring_copy(src, kd, dr, h + 1))
            elif h == 3:
                if kd == 0:
                    start(ring_copy(src, 3 + dr, dr, 4))
                elif kd == 1 + dr:
                    start(ring_copy(src, kd, dr, 4))

    def to_sib(src, dst, s, r):
        return pltpu.make_async_remote_copy(
            src_ref=src, dst_ref=dst, send_sem=s, recv_sem=r, device_id={"ctx": sib}, device_id_type=MESH
        )

    def decode(r):
        qr = dq_rows[16 * r : 16 * r + 16].astype(BF16)
        s = lax.dot_general(qr, cache_v[0, r], NT, preferred_element_type=F32)
        ek = jnp.exp2(column(ce[0, r])) * SCALE2
        ev = jnp.exp2(column(ce[1, r]))
        length = clen[0, r]
        lane = lax.broadcasted_iota(jnp.int32, (16, CBLK), 1)
        cols = []
        for b in range(CACHE // CBLK):
            x = s[:, b * CBLK : (b + 1) * CBLK] * ek[b : b + 1, :]
            cols.append(jnp.where(lane < length - b * CBLK, x, NEG))
        kn = dn[0, r : r + 1].astype(F32)
        vn = dn[1, r : r + 1].astype(F32)
        own = jnp.sum(qr.astype(F32) * kn, axis=1, keepdims=True) * SCALE2
        top = cols[0]
        for x in cols[1:]:
            top = jnp.maximum(top, x)
        top = jnp.maximum(jnp.max(top, axis=1, keepdims=True), own)
        tot = jnp.zeros((16, CBLK), F32)
        pv = []
        for b, x in enumerate(cols):
            e = jnp.exp2(x - top)
            tot = tot + e
            pv.append((e * ev[b : b + 1, :]).astype(BF16))
        own = jnp.exp2(own - top)
        total = jnp.sum(tot, axis=1, keepdims=True) + own
        o = jnp.dot(jnp.concatenate(pv, axis=1), cache_v[1, r], preferred_element_type=F32)
        o = o + own.astype(BF16).astype(F32) * vn
        ga[core, z, 16 * r : 16 * r + 16] = (o / total).astype(BF16)

    def attend(blocks, half, first=False, masked=False, each=None):
        for c in range(ROWS // CHUNK):
            rows = pl.ds(half * ROWS + c * CHUNK, CHUNK)
            qc = q_rows[rows]
            keys = jnp.concatenate([b[0][...] for b in blocks], axis=0)
            vals = jnp.concatenate([b[1][...] for b in blocks], axis=0)
            n = keys.shape[0]
            s = lax.dot_general(qc, keys, NT, preferred_element_type=F32)
            if masked:
                col = lax.broadcasted_iota(jnp.int32, (CHUNK, n), 1)
                key = (col // TOK) * (2 * TOK) + lax.rem(col, TOK) + core * TOK
                tok = lax.rem(lax.broadcasted_iota(jnp.int32, (CHUNK, n), 0), TOK) + (sib if half else p) * TOK
                s = jnp.where(key <= tok, s, NEG)
            top = jnp.max(s, axis=1, keepdims=True) * SCALE2
            if not first:
                before = m_ref[rows]
                top = jnp.maximum(before[:, 0:1], top)
            e = jnp.exp2(s * SCALE2 - top).astype(BF16)
            vals = jnp.concatenate([vals, jnp.ones((n, HD), BF16)], axis=1)
            o = jnp.dot(e, vals, preferred_element_type=F32)
            if not first:
                keep = jnp.exp2(before - top)
                o = o + acc_ref[rows] * jnp.concatenate([keep, keep], axis=1)
            top = jnp.broadcast_to(top, (CHUNK, HD))
            if each is not None:
                each(c, o, top)
            else:
                acc_ref[rows] = o
                m_ref[rows] = top

    def pref(src):
        return (gp.at[src, 0], gp.at[src, 1])

    post(1)
    post(2)
    ld[0].wait()
    ld[1].wait()
    gn[z, 0:TOK] = nraw[0]
    gn[z, TOK + FAC : NEWR] = nraw[1]
    fk = jnp.exp2(-column(ne[0]))
    fv = jnp.exp2(-column(ne[1]))
    fac = jnp.concatenate([fk, fv, jnp.zeros((8, 1), F32)], axis=0)
    gn[z, TOK : TOK + FAC] = jnp.broadcast_to(fac, (FAC, HD)).astype(BF16)
    post(0)
    part_s[...] = jnp.zeros(part_s.shape, F32)
    ld[8].wait()
    for h in range(GROUP):
        q_rows[h * TOK : (h + 1) * TOK, :] = q_in[:, h * HD : (h + 1) * HD]
    q_copy = to_sib(q_rows.at[0:ROWS], q_rows.at[ROWS : 2 * ROWS], q_s.at[0], q_r.at[0])
    start(q_copy)
    ld[3].wait()
    x = dq_in[...].astype(F32)
    dq_rows[...] = jnp.zeros((32, HD), F32)
    for r in range(2):
        for h in range(GROUP):
            dq_rows[16 * r + h : 16 * r + h + 1, :] = x[r : r + 1, h * HD : (h + 1) * HD]
    for i in (4, 5, 6, 7, 12):
        ld[i].wait()
    decode(0)
    decode(1)
    for d in range(1, 8):
        c = pltpu.make_async_remote_copy(
            src_ref=ga.at[core, z], dst_ref=ga.at[core, z], send_sem=at_s.at[d], recv_sem=at_r.at[d],
            device_id={"ctx": lax.rem(p + 2 * d, N_CTX)}, device_id_type=MESH,
        )
        start(c)
    pump(1, 0)
    ld[2].wait()
    attend([pref(z)], 0, first=True)
    pump(1, 1)
    pump(1, 2)
    q_copy.wait_recv()
    attend([pref(z)], 1, first=True)
    pump(2, 0)
    one = [pref(origin(0, 1)), pref(origin(1, 1))]
    attend(one, 0)

    for d in range(1, 8):
        zs = lax.rem(z + 8 - d, 8)
        to_sib(ga.at[core, zs], ga.at[core, zs], at_s.at[d], at_r.at[d]).wait_recv()
    start(to_sib(ga.at[core], ga.at[core], at_s.at[0], at_r.at[0]))
    pump(2, 1)
    pump(2, 2)
    pump(3, 0)
    attend(one, 1)
    to_sib(ga.at[1 - core], ga.at[1 - core], at_s.at[0], at_r.at[0]).wait_recv()
    ld[9].wait()
    for cc in range(2):
        for zz in range(8):
            at0 = (2 * zz + cc) * 32
            gaf[at0 : at0 + 32, :] = ga[cc, zz].astype(F32)
    a = jnp.concatenate([gaf[pl.ds(h, 32, stride=16), :] for h in range(GROUP)], axis=1).astype(BF16)
    terms = jnp.dot(a, w_v[...], preferred_element_type=F32)
    for t in range(N_TP):
        t_out[t, 0:4, :] = terms[4 * t : 4 * t + 4, 0 : DOUT // 2]
        t_out[t, 4:8, :] = terms[4 * t : 4 * t + 4, DOUT // 2 : DOUT]
    for d in range(1, N_TP):
        to = lax.rem(tp + d, N_TP)
        c = pltpu.make_async_remote_copy(
            src_ref=t_out.at[to], dst_ref=t_in.at[tp], send_sem=tp_s.at[d], recv_sem=tp_r.at[d],
            device_id={"tp": to}, device_id_type=MESH,
        )
        start(c)
    two = [pref(origin(0, 2)), pref(origin(1, 2))]
    attend(two, 0)
    pump(3, 1)
    pump(3, 2)
    pump(4, 0)

    ships = []
    ld[11].wait()
    for o, owner in enumerate((p, sib)):
        for j in range(4):
            src = lax.rem(owner + N_CTX - shift[role, j], N_CTX)
            mine = lax.rem(src, 2) == core
            f = gn[src // 2, TOK : TOK + FAC].astype(F32)
            for k in range(2):
                at0 = k * (TOK + FAC) + 16 * j
                raw = gn[src // 2, at0 : at0 + 16].astype(F32)
                code = raw * f[4 * k + j : 4 * k + j + 1, :]
                ship_out[o, k, 16 * j : 16 * j + 16] = jnp.where(mine, code, 0.0).astype(BF16)
        c = pltpu.make_async_remote_copy(
            src_ref=ship_out.at[o], dst_ref=ship_in.at[o], send_sem=sh_s.at[o], recv_sem=sh_r.at[o],
            device_id={"role": 1 - role, "ctx": owner}, device_id_type=MESH,
        )
        start(c)
        ships.append(c)
    eye = lax.broadcasted_iota(jnp.int32, (HD, HD), 0) == lax.broadcasted_iota(jnp.int32, (HD, HD), 1)
    backs = []

    def give(c, o, top):
        part_o[c] = (o[:, 0:HD] / o[:, HD:]).astype(BF16)
        lse = top + jnp.log2(o[:, HD:])
        for b in range(CHUNK // HD):
            x = jnp.where(eye, lse[b * HD : (b + 1) * HD], 0.0)
            part_s[c, b : b + 1, :] = jnp.sum(x, axis=0, keepdims=True)
        c1 = to_sib(part_o.at[c], back_o.at[c], po_s.at[c], po_r.at[c])
        c2 = to_sib(part_s.at[c], back_s.at[c], ps_s.at[c], ps_r.at[c])
        start(c1)
        start(c2)
        backs.append((c1, c2))

    def merge(c, o, top):
        mine = o[:, 0:HD] / o[:, HD:]
        lse = top + jnp.log2(o[:, HD:])
        other = []
        for b in range(CHUNK // HD):
            x = jnp.where(eye, jnp.broadcast_to(back_s[c, b : b + 1, :], (HD, HD)), 0.0)
            other.append(jnp.broadcast_to(jnp.sum(x, axis=1, keepdims=True), (HD, HD)))
        other = jnp.concatenate(other, axis=0)
        peak = jnp.maximum(lse, other)
        wa = jnp.exp2(lse - peak)
        wb = jnp.exp2(other - peak)
        res = ((mine * wa + back_o[c].astype(F32) * wb) / (wa + wb)).astype(BF16)
        for b in range(CHUNK // TOK):
            h = c * (CHUNK // TOK) + b
            out_attn[0, :, h * HD : (h + 1) * HD] = res[b * TOK : (b + 1) * TOK]

    attend(two, 1)
    three = [pref(origin(0, 3)), pref(origin(1, 3))]
    fresh = [(gn.at[i, 0:TOK], gn.at[i, TOK + FAC : NEWR]) for i in range(8)]
    attend(three, 1)
    attend(fresh, 1, masked=True, each=give)
    attend(three, 0)
    attend(fresh, 0, masked=True)

    total = t_out[tp]
    for d in range(1, N_TP):
        frm = lax.rem(tp + N_TP - d, N_TP)
        pltpu.make_async_remote_copy(
            src_ref=t_out.at[frm], dst_ref=t_in.at[frm], send_sem=tp_s.at[d], recv_sem=tp_r.at[d],
            device_id={"tp": frm}, device_id_type=MESH,
        ).wait_recv()
        total = total + t_in[frm]
    ld[10].wait()
    wide = jnp.concatenate([total[0:4], total[4:8]], axis=1)
    out_dec[0] = (res_v[...].astype(F32) + wide).astype(BF16)

    pump(4, 1)
    far = origin(0, 4)
    fars = []
    for i in (0, 1):
        c = to_sib(gp.at[far, :, i * HALF : (i + 1) * HALF], far_v.at[:, i * HALF : (i + 1) * HALF], far_s.at[i], far_r.at[i])
        start(c)
        fars.append(c)
    attend([pref(far)], 0)
    for c in fars:
        c.wait_recv()
    for x in backs:
        for c in x:
            c.wait_recv()
    attend([(far_v.at[0], far_v.at[1])], 0, each=merge)
    for c in ships:
        c.wait_recv()
    out_ship[0] = (ship_in[0].astype(F32) + ship_in[1].astype(F32)).astype(BF16)
    for c in sends:
        c.wait_send()


def hand_out(*refs):
    srcs, dsts, sem = refs[:3], refs[3:6], refs[6]
    cs = [pltpu.make_async_copy(a, b, sem.at[i]) for i, (a, b) in enumerate(zip(srcs, dsts))]
    for c in cs:
        c.start()
    for c in cs:
        c.wait()


def per_device(*args):
    args = list(args)
    args[3] = jnp.swapaxes(args[3], -1, -2)
    args[7] = jnp.swapaxes(args[7], -1, -2)
    out = main(*args)
    return pl.pallas_call(
        hand_out,
        out_shape=tuple(pltpu.HBM(x.shape, x.dtype) for x in out),
        in_specs=[pl.BlockSpec(memory_space=pltpu.VMEM)] * 3,
        out_specs=(pl.BlockSpec(memory_space=pltpu.HBM),) * 3,
        scratch_shapes=[pltpu.SemaphoreType.DMA((3,))],
    )(*[pltpu.with_memory_space_constraint(x, pltpu.VMEM) for x in out])


def main(*args):
    hb = pl.BlockSpec(memory_space=pltpu.HBM)
    dma = pltpu.SemaphoreType.DMA
    args = [pltpu.with_memory_space_constraint(a, pltpu.HBM) for a in args]
    return pl.pallas_call(
        kernel,
        out_shape=(
            pltpu.VMEM((1, TOK, GROUP * HD), BF16),
            pltpu.VMEM((1, 2, TOK, HD), BF16),
            pltpu.VMEM((1, 4, DOUT), BF16),
        ),
        in_specs=[hb] * len(args),
        out_specs=(pl.BlockSpec(memory_space=pltpu.VMEM),) * 3,
        scratch_shapes=[
            pltpu.VMEM((8, 2, PRE, HD), BF16),
            pltpu.VMEM((8, NEWR, HD), BF16),
            pltpu.VMEM((2, TOK, HD), BF16),
            pltpu.VMEM((2, 1, 4), jnp.int32),
            pltpu.VMEM((TOK, GROUP * HD), BF16),
            pltpu.VMEM((2 * ROWS, HD), BF16),
            pltpu.VMEM((2 * ROWS, HD), F32),
            pltpu.VMEM((2 * ROWS, 2 * HD), F32),
            pltpu.VMEM((2, GROUP * HD), BF16),
            pltpu.VMEM((32, HD), F32),
            pltpu.VMEM((2, 2, CACHE, HD), BF16),
            pltpu.VMEM((2, 2, 1, CACHE // CBLK), jnp.int32),
            pltpu.VMEM((2, 2, HD), BF16),
            pltpu.VMEM((2, 8, 32, HD), BF16),
            pltpu.VMEM((512, HD), F32),
            pltpu.VMEM((GROUP * HD, DOUT), BF16),
            pltpu.VMEM((N_TP, 8, DOUT // 2), F32),
            pltpu.VMEM((N_TP, 8, DOUT // 2), F32),
            pltpu.VMEM((4, DOUT), BF16),
            pltpu.VMEM((2, 2, TOK, HD), BF16),
            pltpu.VMEM((2, 2, TOK, HD), BF16),
            pltpu.VMEM((ROWS // CHUNK, CHUNK, HD), BF16),
            pltpu.VMEM((ROWS // CHUNK, 8, HD), F32),
            pltpu.VMEM((ROWS // CHUNK, CHUNK, HD), BF16),
            pltpu.VMEM((ROWS // CHUNK, 8, HD), F32),
            pltpu.VMEM((2, PRE, HD), BF16),
            pltpu.SMEM((2, 4), jnp.int32),
            pltpu.SMEM((1, 2), jnp.int32),
            dma((13,)),
            dma((22,)), dma((22,)),
            dma((1,)), dma((1,)),
            dma((8,)), dma((8,)),
            dma((8,)), dma((8,)),
            dma((2,)), dma((2,)),
            dma((3,)), dma((3,)),
            dma((3,)), dma((3,)),
            dma((2,)), dma((2,)),
        ],
        compiler_params=pltpu.CompilerParams(
            collective_id=0, has_side_effects=True, vmem_limit_bytes=48 * 2**20
        ),
    )(*args)


def solution(mesh):
    placed = (
        P("role", "ctx", "tp"),
        P("role", None, "ctx", "tp"),
        P("role", None, "ctx", "tp"),
        P("role", None, "ctx", "tp"),
        P(),
        P("role", "ctx", "tp"),
        P("role", None, "ctx", None, "tp"),
        P("role", None, "ctx", None, "tp"),
        P("role", "ctx"),
        P("role", None, "ctx", "tp"),
        P("tp", "ctx"),
        P("role", "tp", "ctx"),
    )
    return jax.shard_map(
        per_device,
        mesh=mesh,
        in_specs=placed,
        out_specs=(P("role", "ctx", "tp"), P("role", None, "ctx", "tp"), P("role", "tp", "ctx")),
        check_vma=False,
    )
```

```python
import jax
import jax.numpy as jnp
from jax import lax
from jax.experimental import pallas as pl
from jax.experimental.pallas import tpu as pltpu
from jax.sharding import PartitionSpec as P

MESH = pl.DeviceIdType.MESH
BF16 = jnp.bfloat16
F32 = jnp.float32
HD = 128
GROUP = 12
TOK = 64
PRE = 256
HALF = PRE // 2
ROWS = GROUP * TOK
N_CTX = 16
N_TP = 8
CACHE = 2048
CBLK = 128
DOUT = 768
LOG2E = 1.4426950408889634
SCALE2 = HD**-0.5 * LOG2E
CHUNK = 256
NEG = -1e30
NT = (((1,), (1,)), ((), ()))


def column(row):
    n = row.shape[1]
    wide = jnp.broadcast_to(row.astype(F32), (n, n))
    on = lax.broadcasted_iota(jnp.int32, (n, n), 0) == lax.broadcasted_iota(jnp.int32, (n, n), 1)
    return jnp.sum(jnp.where(on, wide, 0.0), axis=1, keepdims=True)


def kernel(
    q_hbm, prefix, new, nexp, shift_in, dq, cache, cexp, clen_in, dnew, w, resid,
    out_attn, out_ship, out_dec,
    gp, gn, ne, q_in, q_rows, m_ref, acc_ref,
    dq_in, dq_rows, cache_v, ce, dn, ga, gb, gaf, w_v, t_out, t_in, res_v, ship_out, ship_in,
    part_o, part_s, back_o, back_s, far_v, shift, clen,
    lsem, ring_s, ring_r, q_s, q_r, at_s, at_r, tp_s, tp_r, sh_s, sh_r, po_s, po_r, ps_s, ps_r, far_s, far_r, near, nearer,
):
    role, p, tp = lax.axis_index("role"), lax.axis_index("ctx"), lax.axis_index("tp")
    core = lax.rem(p, 2)
    z = p // 2
    right, left = lax.rem(p + 2, N_CTX), lax.rem(p + N_CTX - 2, N_CTX)
    sib = p + 1 - 2 * core

    y, x_lo = lax.rem(tp, 4), tp // 4
    beside = [{"tp": x_lo * 4 + lax.rem(y + 1, 4)}, {"tp": x_lo * 4 + lax.rem(y + 3, 4)}, {"tp": (1 - x_lo) * 4 + y}]
    bar = pltpu.get_barrier_semaphore()
    for d in [{"ctx": right}, {"ctx": left}, {"ctx": sib}, {"role": 1 - role}] + beside:
        pl.semaphore_signal(bar, inc=1, device_id=d, device_id_type=MESH)

    loads = [
        (new.at[0], gn.at[z]), (nexp.at[0], ne), (prefix.at[0], gp.at[z]),
        (dq.at[0], dq_in), (cexp.at[0], ce), (dnew.at[0], dn),
        (cache.at[0, 0], cache_v.at[0]), (cache.at[0, 1], cache_v.at[1]),
        (q_hbm.at[0], q_in), (w, w_v), (resid.at[0], res_v), (shift_in, shift), (clen_in, clen),
    ]
    ld = [pltpu.make_async_copy(s, d, lsem.at[i]) for i, (s, d) in enumerate(loads)]
    for c in ld:
        c.start()

    pl.semaphore_wait(bar, 7)

    dev = (right, left)
    kinds = {h: ((0, 1, 2), (0, 2, 1)) for h in (1, 2, 3)}
    kinds[4] = ((3, 1), (4, 2))
    slot = {}
    for dr in (0, 1):
        for h in (1, 2, 3, 4):
            for kd in kinds[h][dr]:
                slot[(dr, h, kd)] = len(slot)

    def part(src, kd):
        if kd == 0:
            return gn.at[src]
        if kd == 1:
            return gp.at[src, :, 0:HALF]
        if kd == 2:
            return gp.at[src, :, HALF:PRE]
        if kd == 3:
            return gn.at[src, 0]
        return gn.at[src, 1]

    def origin(dr, h):
        return lax.rem(z + (8 - h if dr == 0 else h), 8)

    def ring_copy(src, kd, dr, h, held=None):
        i = slot[(dr, h, kd)]
        return pltpu.make_async_remote_copy(
            src_ref=part(src, kd) if held is None else held, dst_ref=part(src, kd), send_sem=ring_s.at[i], recv_sem=ring_r.at[i],
            device_id={"ctx": dev[dr]}, device_id_type=MESH,
        )

    sends = []

    def start(c):
        c.start()
        sends.append(c)

    def post(j):
        for dr in (0, 1):
            kd = kinds[1][dr][j]
            src = new.at[0] if j == 0 else prefix.at[0, :, 0:HALF] if kd == 1 else prefix.at[0, :, HALF:PRE]
            start(ring_copy(z, kd, dr, 1, src))

    def pump(h, j):
        for dr in (0, 1):
            kd = kinds[h][dr][j]
            src = origin(dr, h)
            ring_copy(src, kd, dr, h).wait_recv()
            if h < 3:
                start(ring_copy(src, kd, dr, h + 1))
            elif h == 3:
                if kd == 0:
                    start(ring_copy(src, 3 + dr, dr, 4))
                elif kd == 1 + dr:
                    start(ring_copy(src, kd, dr, 4))

    def to_sib(src, dst, s, r):
        return pltpu.make_async_remote_copy(
            src_ref=src, dst_ref=dst, send_sem=s, recv_sem=r, device_id={"ctx": sib}, device_id_type=MESH
        )

    def decode(r):
        qr = dq_rows[16 * r : 16 * r + 16].astype(BF16)
        s = lax.dot_general(qr, cache_v[0, r], NT, preferred_element_type=F32)
        ek = jnp.exp2(column(ce[0, r])) * SCALE2
        ev = jnp.exp2(column(ce[1, r]))
        length = clen[0, r]
        lane = lax.broadcasted_iota(jnp.int32, (16, CBLK), 1)
        cols = []
        for b in range(CACHE // CBLK):
            x = s[:, b * CBLK : (b + 1) * CBLK] * ek[b : b + 1, :]
            cols.append(jnp.where(lane < length - b * CBLK, x, NEG))
        kn = dn[0, r : r + 1].astype(F32)
        vn = dn[1, r : r + 1].astype(F32)
        own = jnp.sum(qr.astype(F32) * kn, axis=1, keepdims=True) * SCALE2
        top = cols[0]
        for x in cols[1:]:
            top = jnp.maximum(top, x)
        top = jnp.maximum(jnp.max(top, axis=1, keepdims=True), own)
        tot = jnp.zeros((16, CBLK), F32)
        pv = []
        for b, x in enumerate(cols):
            e = jnp.exp2(x - top)
            tot = tot + e
            pv.append((e * ev[b : b + 1, :]).astype(BF16))
        own = jnp.exp2(own - top)
        total = jnp.sum(tot, axis=1, keepdims=True) + own
        o = jnp.dot(jnp.concatenate(pv, axis=1), cache_v[1, r], preferred_element_type=F32)
        o = o + own.astype(BF16).astype(F32) * vn
        fac = jnp.concatenate([jnp.zeros((12, 1), F32), jnp.exp2(-column(ne[r]))], axis=0)
        row = lax.broadcasted_iota(jnp.int32, (16, HD), 0)
        ga[z, 16 * r : 16 * r + 16] = jnp.where(row < GROUP, o / total, fac).astype(BF16)

    def attend(blocks, half, first=False, fresh=False, each=None):
        if fresh:
            blocks = blocks + [(gn.at[i, 0], gn.at[i, 1]) for i in range(8)]
        keys = jnp.concatenate([b[0][...] for b in blocks], axis=0)
        n = keys.shape[0]
        vals = jnp.concatenate([b[1][...] for b in blocks], axis=0)
        vals = jnp.concatenate([vals, jnp.ones((n, HD), BF16)], axis=1)
        chunks = [pl.ds(half * ROWS + c * CHUNK, CHUNK) for c in range(ROWS // CHUNK)]

        def scores(c):
            s = lax.dot_general(q_rows[chunks[c]], keys, NT, preferred_element_type=F32)
            return [s[:, j : j + HD] for j in range(0, n, HD)]

        s = scores(0)
        for c, rows in enumerate(chunks):
            later = scores(c + 1) if c + 1 < len(chunks) else None
            if fresh:
                lane = lax.broadcasted_iota(jnp.int32, (CHUNK, HD), 1)
                key = (lane // TOK) * (2 * TOK) + lax.rem(lane, TOK) + core * TOK
                tok = lax.rem(lax.broadcasted_iota(jnp.int32, (CHUNK, HD), 0), TOK) + (sib if half else p) * TOK
                for j in range(4):
                    i = len(s) - 4 + j
                    s[i] = jnp.where(key + j * (4 * TOK) <= tok, s[i], NEG)
            top = s[0]
            for x in s[1:]:
                top = jnp.maximum(top, x)
            top = jnp.broadcast_to(jnp.max(top, axis=1, keepdims=True), (CHUNK, HD))
            if not first:
                before = m_ref[rows]
                top = jnp.maximum(before, top)
            e = jnp.concatenate([jnp.exp2((x - top) * SCALE2).astype(BF16) for x in s], axis=1)
            o = jnp.dot(e, vals, preferred_element_type=F32)
            if not first:
                keep = jnp.exp2((before - top) * SCALE2)
                o = o + acc_ref[rows] * jnp.concatenate([keep, keep], axis=1)
            if each is not None:
                each(c, o, top)
            else:
                acc_ref[rows] = o
                m_ref[rows] = top
            s = later

    def pref(src):
        return (gp.at[src, 0], gp.at[src, 1])

    post(0)
    post(1)
    post(2)
    for d in beside + [{"ctx": sib}]:
        pl.semaphore_signal(near, inc=1, device_id=d, device_id_type=MESH)
    part_s[...] = jnp.zeros(part_s.shape, F32)
    ld[8].wait()
    for h in range(GROUP):
        q_rows[h * TOK : (h + 1) * TOK, :] = q_in[:, h * HD : (h + 1) * HD]
    q_copy = to_sib(q_rows.at[0:ROWS], q_rows.at[ROWS : 2 * ROWS], q_s.at[0], q_r.at[0])
    start(q_copy)
    ld[3].wait()
    x = dq_in[...].astype(F32)
    dq_rows[...] = jnp.zeros((32, HD), F32)
    for r in range(2):
        for h in range(GROUP):
            dq_rows[16 * r + h : 16 * r + h + 1, :] = x[r : r + 1, h * HD : (h + 1) * HD]
    for i in (1, 4, 5, 6, 7, 12):
        ld[i].wait()
    decode(0)
    decode(1)

    def at_send(*steps):
        for d in steps:
            c = pltpu.make_async_remote_copy(
                src_ref=ga.at[z], dst_ref=ga.at[z], send_sem=at_s.at[d], recv_sem=at_r.at[d],
                device_id={"ctx": lax.rem(p + 2 * d, N_CTX)}, device_id_type=MESH,
            )
            start(c)

    pump(1, 0)
    at_send(1, 7, 2, 6)
    pump(1, 1)
    pump(1, 2)
    one = [pref(z), pref(origin(0, 1)), pref(origin(1, 1))]
    ld[2].wait()
    attend(one, 0, first=True)
    pump(2, 0)
    at_send(3, 5)
    q_copy.wait_recv()
    attend(one, 1, first=True)
    pump(2, 1)
    pump(2, 2)
    pump(3, 0)
    at_send(4)
    pl.semaphore_wait(near, 4)
    for d in beside:
        pl.semaphore_signal(nearer, inc=1, device_id=d, device_id_type=MESH)
    two = [pref(origin(0, 2)), pref(origin(1, 2))]
    attend(two, 0)
    attend(two, 1)
    pump(4, 0)
    ld[0].wait()

    for d in range(1, 8):
        zs = lax.rem(z + 8 - d, 8)
        to_sib(ga.at[zs], ga.at[zs], at_s.at[d], at_r.at[d]).wait_recv()
    start(to_sib(ga, gb, at_s.at[0], at_r.at[0]))
    ships = []
    ld[11].wait()
    for o, owner in enumerate((p, sib)):
        for j in range(4):
            src = lax.rem(owner + N_CTX - shift[role, j], N_CTX)
            mine = lax.rem(src, 2) == core
            for k in range(2):
                f = ga[src // 2, 16 * k : 16 * k + 16].astype(F32)
                raw = gn[src // 2, k, 16 * j : 16 * j + 16].astype(F32)
                code = raw * f[GROUP + j : GROUP + j + 1, :]
                ship_out[o, k, 16 * j : 16 * j + 16] = jnp.where(mine, code, 0.0).astype(BF16)
        c = pltpu.make_async_remote_copy(
            src_ref=ship_out.at[o], dst_ref=ship_in.at[o], send_sem=sh_s.at[o], recv_sem=sh_r.at[o],
            device_id={"role": 1 - role, "ctx": owner}, device_id_type=MESH,
        )
        start(c)
        ships.append(c)
    pump(3, 1)
    pump(3, 2)
    pl.semaphore_wait(nearer, 3)
    to_sib(ga, gb, at_s.at[0], at_r.at[0]).wait_recv()
    ld[9].wait()
    for zz in range(8):
        gaf[pl.ds(pl.multiple_of((2 * zz + core) * 32, 32), 32), :] = ga[zz].astype(F32)
        gaf[pl.ds(pl.multiple_of((2 * zz + 1 - core) * 32, 32), 32), :] = gb[zz].astype(F32)
    a = jnp.concatenate([gaf[pl.ds(h, 32, stride=16), :] for h in range(GROUP)], axis=1).astype(BF16)
    terms = jnp.dot(a, w_v[...], preferred_element_type=F32)
    for t in range(N_TP):
        t_out[t, 0:4, :] = terms[4 * t : 4 * t + 4, 0 : DOUT // 2]
        t_out[t, 4:8, :] = terms[4 * t : 4 * t + 4, DOUT // 2 : DOUT]
    for d in range(1, N_TP):
        to = lax.rem(tp + d, N_TP)
        c = pltpu.make_async_remote_copy(
            src_ref=t_out.at[to], dst_ref=t_in.at[tp], send_sem=tp_s.at[d], recv_sem=tp_r.at[d],
            device_id={"tp": to}, device_id_type=MESH,
        )
        start(c)
    eye = lax.broadcasted_iota(jnp.int32, (HD, HD), 0) == lax.broadcasted_iota(jnp.int32, (HD, HD), 1)
    backs = []

    def give(c, o, top):
        part_o[c] = (o[:, 0:HD] / o[:, HD:]).astype(BF16)
        lse = top * SCALE2 + jnp.log2(o[:, HD:])
        for b in range(CHUNK // HD):
            x = jnp.where(eye, lse[b * HD : (b + 1) * HD], 0.0)
            part_s[c, b : b + 1, :] = jnp.sum(x, axis=0, keepdims=True)
        c1 = to_sib(part_o.at[c], back_o.at[c], po_s.at[c], po_r.at[c])
        c2 = to_sib(part_s.at[c], back_s.at[c], ps_s.at[c], ps_r.at[c])
        start(c1)
        start(c2)
        backs.append((c1, c2))

    def merge(c, o, top):
        mine = o[:, 0:HD] / o[:, HD:]
        lse = top * SCALE2 + jnp.log2(o[:, HD:])
        other = []
        for b in range(CHUNK // HD):
            x = jnp.where(eye, jnp.broadcast_to(back_s[c, b : b + 1, :], (HD, HD)), 0.0)
            other.append(jnp.broadcast_to(jnp.sum(x, axis=1, keepdims=True), (HD, HD)))
        other = jnp.concatenate(other, axis=0)
        peak = jnp.maximum(lse, other)
        wa = jnp.exp2(lse - peak)
        wb = jnp.exp2(other - peak)
        res = ((mine * wa + back_o[c].astype(F32) * wb) / (wa + wb)).astype(BF16)
        for b in range(CHUNK // TOK):
            h = c * (CHUNK // TOK) + b
            out_attn[0, :, h * HD : (h + 1) * HD] = res[b * TOK : (b + 1) * TOK]

    three = [pref(origin(0, 3)), pref(origin(1, 3))]
    attend(three, 1, fresh=True, each=give)
    attend(three, 0, fresh=True)
    pump(4, 1)
    far = origin(0, 4)
    fars = []
    for i in (0, 1):
        c = to_sib(gp.at[far, :, i * HALF : (i + 1) * HALF], far_v.at[:, i * HALF : (i + 1) * HALF], far_s.at[i], far_r.at[i])
        start(c)
        fars.append(c)
    for x in backs:
        for c in x:
            c.wait_recv()
    for c in fars:
        c.wait_recv()
    attend([pref(far), (far_v.at[0], far_v.at[1])], 0, each=merge)
    total = t_out[tp]
    for d in range(1, N_TP):
        frm = lax.rem(tp + N_TP - d, N_TP)
        pltpu.make_async_remote_copy(
            src_ref=t_out.at[frm], dst_ref=t_in.at[frm], send_sem=tp_s.at[d], recv_sem=tp_r.at[d],
            device_id={"tp": frm}, device_id_type=MESH,
        ).wait_recv()
        total = total + t_in[frm]
    ld[10].wait()
    wide = jnp.concatenate([total[0:4], total[4:8]], axis=1)
    out_dec[0] = (res_v[...].astype(F32) + wide).astype(BF16)

    for c in ships:
        c.wait_recv()
    out_ship[0] = (ship_in[0].astype(F32) + ship_in[1].astype(F32)).astype(BF16)
    for c in sends:
        c.wait_send()


def hand_out(*refs):
    srcs, dsts, sem = refs[:3], refs[3:6], refs[6]
    cs = [pltpu.make_async_copy(a, b, sem.at[i]) for i, (a, b) in enumerate(zip(srcs, dsts))]
    for c in cs:
        c.start()
    for c in cs:
        c.wait()


def per_device(*args):
    args = list(args)
    args[3] = jnp.swapaxes(args[3], -1, -2)
    args[7] = jnp.swapaxes(args[7], -1, -2)
    out = main(*args)
    return pl.pallas_call(
        hand_out,
        out_shape=tuple(pltpu.HBM(x.shape, x.dtype) for x in out),
        in_specs=[pl.BlockSpec(memory_space=pltpu.VMEM)] * 3,
        out_specs=(pl.BlockSpec(memory_space=pltpu.HBM),) * 3,
        scratch_shapes=[pltpu.SemaphoreType.DMA((3,))],
    )(*[pltpu.with_memory_space_constraint(x, pltpu.VMEM) for x in out])


def main(*args):
    hb = pl.BlockSpec(memory_space=pltpu.HBM)
    dma = pltpu.SemaphoreType.DMA
    args = [pltpu.with_memory_space_constraint(a, pltpu.HBM) for a in args]
    return pl.pallas_call(
        kernel,
        out_shape=(
            pltpu.VMEM((1, TOK, GROUP * HD), BF16),
            pltpu.VMEM((1, 2, TOK, HD), BF16),
            pltpu.VMEM((1, 4, DOUT), BF16),
        ),
        in_specs=[hb] * len(args),
        out_specs=(pl.BlockSpec(memory_space=pltpu.VMEM),) * 3,
        scratch_shapes=[
            pltpu.VMEM((8, 2, PRE, HD), BF16),
            pltpu.VMEM((8, 2, TOK, HD), BF16),
            pltpu.VMEM((2, 1, 4), jnp.int32),
            pltpu.VMEM((TOK, GROUP * HD), BF16),
            pltpu.VMEM((2 * ROWS, HD), BF16),
            pltpu.VMEM((2 * ROWS, HD), F32),
            pltpu.VMEM((2 * ROWS, 2 * HD), F32),
            pltpu.VMEM((2, GROUP * HD), BF16),
            pltpu.VMEM((32, HD), F32),
            pltpu.VMEM((2, 2, CACHE, HD), BF16),
            pltpu.VMEM((2, 2, 1, CACHE // CBLK), jnp.int32),
            pltpu.VMEM((2, 2, HD), BF16),
            pltpu.VMEM((8, 32, HD), BF16),
            pltpu.VMEM((8, 32, HD), BF16),
            pltpu.VMEM((512, HD), F32),
            pltpu.VMEM((GROUP * HD, DOUT), BF16),
            pltpu.VMEM((N_TP, 8, DOUT // 2), F32),
            pltpu.VMEM((N_TP, 8, DOUT // 2), F32),
            pltpu.VMEM((4, DOUT), BF16),
            pltpu.VMEM((2, 2, TOK, HD), BF16),
            pltpu.VMEM((2, 2, TOK, HD), BF16),
            pltpu.VMEM((ROWS // CHUNK, CHUNK, HD), BF16),
            pltpu.VMEM((ROWS // CHUNK, 8, HD), F32),
            pltpu.VMEM((ROWS // CHUNK, CHUNK, HD), BF16),
            pltpu.VMEM((ROWS // CHUNK, 8, HD), F32),
            pltpu.VMEM((2, PRE, HD), BF16),
            pltpu.SMEM((2, 4), jnp.int32),
            pltpu.SMEM((1, 2), jnp.int32),
            dma((13,)),
            dma((22,)), dma((22,)),
            dma((1,)), dma((1,)),
            dma((8,)), dma((8,)),
            dma((8,)), dma((8,)),
            dma((2,)), dma((2,)),
            dma((3,)), dma((3,)),
            dma((3,)), dma((3,)),
            dma((2,)), dma((2,)),
            pltpu.SemaphoreType.REGULAR,
            pltpu.SemaphoreType.REGULAR,
        ],
        compiler_params=pltpu.CompilerParams(
            collective_id=0, has_side_effects=True, vmem_limit_bytes=48 * 2**20
        ),
    )(*args)


def solution(mesh):
    placed = (
        P("role", "ctx", "tp"),
        P("role", None, "ctx", "tp"),
        P("role", None, "ctx", "tp"),
        P("role", None, "ctx", "tp"),
        P(),
        P("role", "ctx", "tp"),
        P("role", None, "ctx", None, "tp"),
        P("role", None, "ctx", None, "tp"),
        P("role", "ctx"),
        P("role", None, "ctx", "tp"),
        P("tp", "ctx"),
        P("role", "tp", "ctx"),
    )
    return jax.shard_map(
        per_device,
        mesh=mesh,
        in_specs=placed,
        out_specs=(P("role", "ctx", "tp"), P("role", None, "ctx", "tp"), P("role", "tp", "ctx")),
        check_vma=False,
    )
```

```python
import jax
import jax.numpy as jnp
from jax import lax
from jax.experimental import pallas as pl
from jax.experimental.pallas import tpu as pltpu
from jax.sharding import PartitionSpec as P

MESH = pl.DeviceIdType.MESH
BF16 = jnp.bfloat16
F32 = jnp.float32
HD = 128
GROUP = 12
TOK = 64
PRE = 256
HALF = PRE // 2
ROWS = GROUP * TOK
N_CTX = 16
N_TP = 8
CACHE = 2048
CBLK = 128
DOUT = 768
LOG2E = 1.4426950408889634
SCALE2 = HD**-0.5 * LOG2E
CHUNK = 256
NEG = -1e30
NT = (((1,), (1,)), ((), ()))


def column(row):
    n = row.shape[1]
    wide = jnp.broadcast_to(row.astype(F32), (n, n))
    on = lax.broadcasted_iota(jnp.int32, (n, n), 0) == lax.broadcasted_iota(jnp.int32, (n, n), 1)
    return jnp.sum(jnp.where(on, wide, 0.0), axis=1, keepdims=True)


def kernel(
    q_hbm, prefix, new, nexp, shift_in, dq, cache, cexp, clen_in, dnew, w, resid,
    out_attn, out_ship, out_dec,
    gp, gn, ne, q_in, q_rows, m_ref, acc_ref,
    dq_in, dq_rows, cache_v, ce, dn, ga, gb, gaf, w_v, t_out, t_in, res_v, ship_out, ship_in,
    part_o, part_s, back_o, back_s, far_v, shift, clen,
    lsem, ring_s, ring_r, q_s, q_r, at_s, at_r, tp_s, tp_r, sh_s, sh_r, po_s, po_r, ps_s, ps_r, far_s, far_r, near, z_sem,
):
    role, p, tp = lax.axis_index("role"), lax.axis_index("ctx"), lax.axis_index("tp")
    core = lax.rem(p, 2)
    z = p // 2
    right, left = lax.rem(p + 2, N_CTX), lax.rem(p + N_CTX - 2, N_CTX)
    sib = p + 1 - 2 * core

    y, x = lax.rem(tp, 4), 2 * role + tp // 4
    beside = [
        (x < 3, {"role": (x + 1) // 2, "tp": lax.rem(x + 1, 2) * 4 + y}),
        (x > 0, {"role": (x - 1) // 2, "tp": lax.rem(x + 3, 2) * 4 + y}),
        (y < 3, {"tp": tp + 1}),
        (y > 0, {"tp": tp - 1}),
    ]
    count = sum(there.astype(jnp.int32) for there, _ in beside)

    def tell(sem):
        for there, d in beside:

            @pl.when(there)
            def _(d=d):
                pl.semaphore_signal(sem, inc=1, device_id=d, device_id_type=MESH)

    bar = pltpu.get_barrier_semaphore()
    for d in ({"ctx": right}, {"ctx": left}, {"ctx": sib}):
        pl.semaphore_signal(bar, inc=1, device_id=d, device_id_type=MESH)
    tell(bar)

    loads = [
        (new.at[0], gn.at[z]), (nexp.at[0], ne), (prefix.at[0], gp.at[z]),
        (dq.at[0], dq_in), (cexp.at[0], ce), (dnew.at[0], dn),
        (cache.at[0, 0], cache_v.at[0]), (cache.at[0, 1], cache_v.at[1]),
        (q_hbm.at[0], q_in), (w, w_v), (resid.at[0], res_v), (shift_in, shift), (clen_in, clen),
    ]
    ld = [pltpu.make_async_copy(s, d, lsem.at[i]) for i, (s, d) in enumerate(loads)]
    pl.semaphore_wait(bar, 3 + count)

    dev = (right, left)
    kinds = {h: ((0, 1, 2), (0, 2, 1)) for h in (1, 2, 3)}
    kinds[4] = ((3, 1), (4, 2))
    slot = {}
    for dr in (0, 1):
        for h in (1, 2, 3, 4):
            for kd in kinds[h][dr]:
                slot[(dr, h, kd)] = len(slot)

    def part(src, kd):
        if kd == 0:
            return gn.at[src]
        if kd == 1:
            return gp.at[src, :, 0:HALF]
        if kd == 2:
            return gp.at[src, :, HALF:PRE]
        if kd == 3:
            return gn.at[src, 0]
        return gn.at[src, 1]

    def origin(dr, h):
        return lax.rem(z + (8 - h if dr == 0 else h), 8)

    def ring_copy(src, kd, dr, h, held=None):
        i = slot[(dr, h, kd)]
        return pltpu.make_async_remote_copy(
            src_ref=part(src, kd) if held is None else held, dst_ref=part(src, kd), send_sem=ring_s.at[i], recv_sem=ring_r.at[i],
            device_id={"ctx": dev[dr]}, device_id_type=MESH,
        )

    sends = []
    done = [0]

    def drain(upto):
        for c in sends[done[0] : upto]:
            c.wait_send()
        done[0] = max(done[0], upto)

    def start(c):
        c.start()
        sends.append(c)

    def post(j):
        for dr in (0, 1):
            kd = kinds[1][dr][j]
            src = new.at[0] if j == 0 else prefix.at[0, :, 0:HALF] if kd == 1 else prefix.at[0, :, HALF:PRE]
            start(ring_copy(z, kd, dr, 1, src))

    def pump(h, j):
        for dr in (0, 1):
            kd = kinds[h][dr][j]
            src = origin(dr, h)
            ring_copy(src, kd, dr, h).wait_recv()
            if h < 3:
                start(ring_copy(src, kd, dr, h + 1))
            elif h == 3:
                if kd == 0:
                    start(ring_copy(src, 3 + dr, dr, 4))
                elif kd == 1 + dr:
                    start(ring_copy(src, kd, dr, 4))

    def to_sib(src, dst, s, r):
        return pltpu.make_async_remote_copy(
            src_ref=src, dst_ref=dst, send_sem=s, recv_sem=r, device_id={"ctx": sib}, device_id_type=MESH
        )

    def decode(r):
        qr = dq_rows[16 * r : 16 * r + 16].astype(BF16)
        s = lax.dot_general(qr, cache_v[0, r], NT, preferred_element_type=F32)
        ek = jnp.exp2(column(ce[0, r])) * SCALE2
        ev = jnp.exp2(column(ce[1, r]))
        length = clen[0, r]
        lane = lax.broadcasted_iota(jnp.int32, (16, CBLK), 1)
        cols = []
        for b in range(CACHE // CBLK):
            x = s[:, b * CBLK : (b + 1) * CBLK] * ek[b : b + 1, :]
            cols.append(jnp.where(lane < length - b * CBLK, x, NEG))
        kn = dn[0, r : r + 1].astype(F32)
        vn = dn[1, r : r + 1].astype(F32)
        own = jnp.sum(qr.astype(F32) * kn, axis=1, keepdims=True) * SCALE2
        top = cols[0]
        for x in cols[1:]:
            top = jnp.maximum(top, x)
        top = jnp.maximum(jnp.max(top, axis=1, keepdims=True), own)
        tot = jnp.zeros((16, CBLK), F32)
        pv = []
        for b, x in enumerate(cols):
            e = jnp.exp2(x - top)
            tot = tot + e
            pv.append((e * ev[b : b + 1, :]).astype(BF16))
        own = jnp.exp2(own - top)
        total = jnp.sum(tot, axis=1, keepdims=True) + own
        o = jnp.dot(jnp.concatenate(pv, axis=1), cache_v[1, r], preferred_element_type=F32)
        o = o + own.astype(BF16).astype(F32) * vn
        fac = jnp.concatenate([jnp.zeros((12, 1), F32), jnp.exp2(-column(ne[r]))], axis=0)
        row = lax.broadcasted_iota(jnp.int32, (16, HD), 0)
        ga[z, 16 * r : 16 * r + 16] = jnp.where(row < GROUP, o / total, fac).astype(BF16)

    def attend(blocks, half, first=False, fresh=False, each=None):
        if fresh:
            blocks = blocks + [(gn.at[i, 0], gn.at[i, 1]) for i in range(8)]
        keys = jnp.concatenate([b[0][...] for b in blocks], axis=0)
        n = keys.shape[0]
        vals = jnp.concatenate([b[1][...] for b in blocks], axis=0)
        vals = jnp.concatenate([vals, jnp.ones((n, HD), BF16)], axis=1)
        chunks = [pl.ds(half * ROWS + c * CHUNK, CHUNK) for c in range(ROWS // CHUNK)]

        def scores(c):
            s = lax.dot_general(q_rows[chunks[c]], keys, NT, preferred_element_type=F32)
            return [s[:, j : j + HD] for j in range(0, n, HD)]

        s = scores(0)
        for c, rows in enumerate(chunks):
            later = scores(c + 1) if c + 1 < len(chunks) else None
            if fresh:
                lane = lax.broadcasted_iota(jnp.int32, (CHUNK, HD), 1)
                key = (lane // TOK) * (2 * TOK) + lax.rem(lane, TOK) + core * TOK
                tok = lax.rem(lax.broadcasted_iota(jnp.int32, (CHUNK, HD), 0), TOK) + (sib if half else p) * TOK
                for j in range(4):
                    i = len(s) - 4 + j
                    s[i] = jnp.where(key + j * (4 * TOK) <= tok, s[i], NEG)
            top = s[0]
            for x in s[1:]:
                top = jnp.maximum(top, x)
            top = jnp.broadcast_to(jnp.max(top, axis=1, keepdims=True), (CHUNK, HD))
            if not first:
                before = m_ref[rows]
                top = jnp.maximum(before, top)
            e = jnp.concatenate([jnp.exp2((x - top) * SCALE2).astype(BF16) for x in s], axis=1)
            o = jnp.dot(e, vals, preferred_element_type=F32)
            if not first:
                keep = jnp.exp2((before - top) * SCALE2)
                o = o + acc_ref[rows] * jnp.concatenate([keep, keep], axis=1)
            if each is not None:
                each(c, o, top)
            else:
                acc_ref[rows] = o
                m_ref[rows] = top
            s = later

    def pref(src):
        return (gp.at[src, 0], gp.at[src, 1])

    post(0)
    post(1)
    post(2)
    along = [{"ctx": right}, {"ctx": left}]
    for d in along:
        pl.semaphore_signal(z_sem.at[0], inc=1, device_id=d, device_id_type=MESH)
    for i in (8, 3, 1, 4, 5, 12, 6, 7, 2, 0, 9, 10, 11):
        ld[i].start()
    tell(near.at[0])
    part_s[...] = jnp.zeros(part_s.shape, F32)
    ld[8].wait()
    for h in range(GROUP):
        q_rows[h * TOK : (h + 1) * TOK, :] = q_in[:, h * HD : (h + 1) * HD]
    q_copy = to_sib(q_rows.at[0:ROWS], q_rows.at[ROWS : 2 * ROWS], q_s.at[0], q_r.at[0])
    start(q_copy)
    ld[3].wait()
    x = dq_in[...].astype(F32)
    dq_rows[...] = jnp.zeros((32, HD), F32)
    for r in range(2):
        for h in range(GROUP):
            dq_rows[16 * r + h : 16 * r + h + 1, :] = x[r : r + 1, h * HD : (h + 1) * HD]
    for i in (1, 4, 5, 6, 7, 12):
        ld[i].wait()
    decode(0)
    decode(1)

    def at_send(*steps):
        for d in steps:
            c = pltpu.make_async_remote_copy(
                src_ref=ga.at[z], dst_ref=ga.at[z], send_sem=at_s.at[d], recv_sem=at_r.at[d],
                device_id={"ctx": lax.rem(p + 2 * d, N_CTX)}, device_id_type=MESH,
            )
            start(c)

    def next_z(i, more):
        pl.semaphore_wait(z_sem.at[i], 2)
        if i < 2:
            for d in along:
                pl.semaphore_signal(z_sem.at[i + 1], inc=1, device_id=d, device_id_type=MESH)
        at_send(*more)

    next_z(0, (1, 7, 2, 6))
    pump(1, 0)
    next_z(1, (3, 5))
    pl.semaphore_wait(near.at[0], count)
    tell(near.at[1])
    pump(1, 1)
    pump(1, 2)
    next_z(2, (4,))
    pl.semaphore_wait(near.at[1], count)
    tell(near.at[2])
    one = [pref(z), pref(origin(0, 1)), pref(origin(1, 1))]
    ld[2].wait()
    attend(one, 0, first=True)
    pump(2, 0)
    q_copy.wait_recv()
    attend(one, 1, first=True)
    old = len(sends)
    pump(2, 1)
    pump(2, 2)
    pump(3, 0)
    two = [pref(origin(0, 2)), pref(origin(1, 2))]
    attend(two, 0)
    for d in range(1, 8):
        zs = lax.rem(z + 8 - d, 8)
        to_sib(ga.at[zs], ga.at[zs], at_s.at[d], at_r.at[d]).wait_recv()
    start(to_sib(ga, gb, at_s.at[0], at_r.at[0]))
    attend(two, 1)
    pump(4, 0)
    ld[0].wait()
    ships = []
    ld[11].wait()
    for o, owner in enumerate((p, sib)):
        for j in range(4):
            src = lax.rem(owner + N_CTX - shift[role, j], N_CTX)
            mine = lax.rem(src, 2) == core
            for k in range(2):
                f = ga[src // 2, 16 * k : 16 * k + 16].astype(F32)
                raw = gn[src // 2, k, 16 * j : 16 * j + 16].astype(F32)
                code = raw * f[GROUP + j : GROUP + j + 1, :]
                ship_out[o, k, 16 * j : 16 * j + 16] = jnp.where(mine, code, 0.0).astype(BF16)
        c = pltpu.make_async_remote_copy(
            src_ref=ship_out.at[o], dst_ref=ship_in.at[o], send_sem=sh_s.at[o], recv_sem=sh_r.at[o],
            device_id={"role": 1 - role, "ctx": owner}, device_id_type=MESH,
        )
        start(c)
        ships.append(c)
    pl.semaphore_wait(near.at[2], count)
    to_sib(ga, gb, at_s.at[0], at_r.at[0]).wait_recv()
    ld[9].wait()
    for zz in range(8):
        gaf[pl.ds(pl.multiple_of((2 * zz + core) * 32, 32), 32), :] = ga[zz].astype(F32)
        gaf[pl.ds(pl.multiple_of((2 * zz + 1 - core) * 32, 32), 32), :] = gb[zz].astype(F32)
    a = jnp.concatenate([gaf[pl.ds(h, 32, stride=16), :] for h in range(GROUP)], axis=1).astype(BF16)
    terms = jnp.dot(a, w_v[...], preferred_element_type=F32)
    for t in range(N_TP):
        t_out[t, 0:4, :] = terms[4 * t : 4 * t + 4, 0 : DOUT // 2]
        t_out[t, 4:8, :] = terms[4 * t : 4 * t + 4, DOUT // 2 : DOUT]
    for d in range(1, N_TP):
        to = lax.rem(tp + d, N_TP)
        c = pltpu.make_async_remote_copy(
            src_ref=t_out.at[to], dst_ref=t_in.at[tp], send_sem=tp_s.at[d], recv_sem=tp_r.at[d],
            device_id={"tp": to}, device_id_type=MESH,
        )
        start(c)
    drain(old)
    old = len(sends)
    pump(3, 1)
    pump(3, 2)
    eye = lax.broadcasted_iota(jnp.int32, (HD, HD), 0) == lax.broadcasted_iota(jnp.int32, (HD, HD), 1)
    backs = []

    def give(c, o, top):
        part_o[c] = (o[:, 0:HD] / o[:, HD:]).astype(BF16)
        lse = top * SCALE2 + jnp.log2(o[:, HD:])
        for b in range(CHUNK // HD):
            x = jnp.where(eye, lse[b * HD : (b + 1) * HD], 0.0)
            part_s[c, b : b + 1, :] = jnp.sum(x, axis=0, keepdims=True)
        c1 = to_sib(part_o.at[c], back_o.at[c], po_s.at[c], po_r.at[c])
        c2 = to_sib(part_s.at[c], back_s.at[c], ps_s.at[c], ps_r.at[c])
        start(c1)
        start(c2)
        backs.append((c1, c2))

    def merge(c, o, top):
        mine = o[:, 0:HD] / o[:, HD:]
        lse = top * SCALE2 + jnp.log2(o[:, HD:])
        other = []
        for b in range(CHUNK // HD):
            x = jnp.where(eye, jnp.broadcast_to(back_s[c, b : b + 1, :], (HD, HD)), 0.0)
            other.append(jnp.broadcast_to(jnp.sum(x, axis=1, keepdims=True), (HD, HD)))
        other = jnp.concatenate(other, axis=0)
        peak = jnp.maximum(lse, other)
        wa = jnp.exp2(lse - peak)
        wb = jnp.exp2(other - peak)
        res = ((mine * wa + back_o[c].astype(F32) * wb) / (wa + wb)).astype(BF16)
        for b in range(CHUNK // TOK):
            h = c * (CHUNK // TOK) + b
            out_attn[0, :, h * HD : (h + 1) * HD] = res[b * TOK : (b + 1) * TOK]

    three = [pref(origin(0, 3)), pref(origin(1, 3))]
    attend(three, 1, fresh=True, each=give)
    attend(three, 0, fresh=True)
    drain(old)

    pump(4, 1)
    far = origin(0, 4)
    fars = []
    for i in (0, 1):
        c = to_sib(gp.at[far, :, i * HALF : (i + 1) * HALF], far_v.at[:, i * HALF : (i + 1) * HALF], far_s.at[i], far_r.at[i])
        start(c)
        fars.append(c)
    for x in backs:
        for c in x:
            c.wait_recv()
    for c in fars:
        c.wait_recv()
    attend([pref(far), (far_v.at[0], far_v.at[1])], 0, each=merge)
    total = t_out[tp]
    for d in range(1, N_TP):
        frm = lax.rem(tp + N_TP - d, N_TP)
        pltpu.make_async_remote_copy(
            src_ref=t_out.at[frm], dst_ref=t_in.at[frm], send_sem=tp_s.at[d], recv_sem=tp_r.at[d],
            device_id={"tp": frm}, device_id_type=MESH,
        ).wait_recv()
        total = total + t_in[frm]
    ld[10].wait()
    wide = jnp.concatenate([total[0:4], total[4:8]], axis=1)
    out_dec[0] = (res_v[...].astype(F32) + wide).astype(BF16)

    for c in ships:
        c.wait_recv()
    out_ship[0] = (ship_in[0].astype(F32) + ship_in[1].astype(F32)).astype(BF16)
    drain(len(sends))


def hand_out(*refs):
    srcs, dsts, sem = refs[:3], refs[3:6], refs[6]
    cs = [pltpu.make_async_copy(a, b, sem.at[i]) for i, (a, b) in enumerate(zip(srcs, dsts))]
    for c in cs:
        c.start()
    for c in cs:
        c.wait()


def per_device(*args):
    args = list(args)
    args[3] = jnp.swapaxes(args[3], -1, -2)
    args[7] = jnp.swapaxes(args[7], -1, -2)
    out = main(*args)
    return pl.pallas_call(
        hand_out,
        out_shape=tuple(pltpu.HBM(x.shape, x.dtype) for x in out),
        in_specs=[pl.BlockSpec(memory_space=pltpu.VMEM)] * 3,
        out_specs=(pl.BlockSpec(memory_space=pltpu.HBM),) * 3,
        scratch_shapes=[pltpu.SemaphoreType.DMA((3,))],
    )(*[pltpu.with_memory_space_constraint(x, pltpu.VMEM) for x in out])


def main(*args):
    hb = pl.BlockSpec(memory_space=pltpu.HBM)
    dma = pltpu.SemaphoreType.DMA
    args = [pltpu.with_memory_space_constraint(a, pltpu.HBM) for a in args]
    return pl.pallas_call(
        kernel,
        out_shape=(
            pltpu.VMEM((1, TOK, GROUP * HD), BF16),
            pltpu.VMEM((1, 2, TOK, HD), BF16),
            pltpu.VMEM((1, 4, DOUT), BF16),
        ),
        in_specs=[hb] * len(args),
        out_specs=(pl.BlockSpec(memory_space=pltpu.VMEM),) * 3,
        scratch_shapes=[
            pltpu.VMEM((8, 2, PRE, HD), BF16),
            pltpu.VMEM((8, 2, TOK, HD), BF16),
            pltpu.VMEM((2, 1, 4), jnp.int32),
            pltpu.VMEM((TOK, GROUP * HD), BF16),
            pltpu.VMEM((2 * ROWS, HD), BF16),
            pltpu.VMEM((2 * ROWS, HD), F32),
            pltpu.VMEM((2 * ROWS, 2 * HD), F32),
            pltpu.VMEM((2, GROUP * HD), BF16),
            pltpu.VMEM((32, HD), F32),
            pltpu.VMEM((2, 2, CACHE, HD), BF16),
            pltpu.VMEM((2, 2, 1, CACHE // CBLK), jnp.int32),
            pltpu.VMEM((2, 2, HD), BF16),
            pltpu.VMEM((8, 32, HD), BF16),
            pltpu.VMEM((8, 32, HD), BF16),
            pltpu.VMEM((512, HD), F32),
            pltpu.VMEM((GROUP * HD, DOUT), BF16),
            pltpu.VMEM((N_TP, 8, DOUT // 2), F32),
            pltpu.VMEM((N_TP, 8, DOUT // 2), F32),
            pltpu.VMEM((4, DOUT), BF16),
            pltpu.VMEM((2, 2, TOK, HD), BF16),
            pltpu.VMEM((2, 2, TOK, HD), BF16),
            pltpu.VMEM((ROWS // CHUNK, CHUNK, HD), BF16),
            pltpu.VMEM((ROWS // CHUNK, 8, HD), F32),
            pltpu.VMEM((ROWS // CHUNK, CHUNK, HD), BF16),
            pltpu.VMEM((ROWS // CHUNK, 8, HD), F32),
            pltpu.VMEM((2, PRE, HD), BF16),
            pltpu.SMEM((2, 4), jnp.int32),
            pltpu.SMEM((1, 2), jnp.int32),
            dma((13,)),
            dma((22,)), dma((22,)),
            dma((1,)), dma((1,)),
            dma((8,)), dma((8,)),
            dma((8,)), dma((8,)),
            dma((2,)), dma((2,)),
            dma((3,)), dma((3,)),
            dma((3,)), dma((3,)),
            dma((2,)), dma((2,)),
            pltpu.SemaphoreType.REGULAR((3,)),
            pltpu.SemaphoreType.REGULAR((3,)),
        ],
        compiler_params=pltpu.CompilerParams(
            collective_id=0, has_side_effects=True, vmem_limit_bytes=48 * 2**20
        ),
    )(*args)


def solution(mesh):
    placed = (
        P("role", "ctx", "tp"),
        P("role", None, "ctx", "tp"),
        P("role", None, "ctx", "tp"),
        P("role", None, "ctx", "tp"),
        P(),
        P("role", "ctx", "tp"),
        P("role", None, "ctx", None, "tp"),
        P("role", None, "ctx", None, "tp"),
        P("role", "ctx"),
        P("role", None, "ctx", "tp"),
        P("tp", "ctx"),
        P("role", "tp", "ctx"),
    )
    return jax.shard_map(
        per_device,
        mesh=mesh,
        in_specs=placed,
        out_specs=(P("role", "ctx", "tp"), P("role", None, "ctx", "tp"), P("role", "tp", "ctx")),
        check_vma=False,
    )
```

```python
import jax
import jax.numpy as jnp
from jax import lax
from jax.experimental import pallas as pl
from jax.experimental.pallas import tpu as pltpu
from jax.sharding import PartitionSpec as P

MESH = pl.DeviceIdType.MESH
BF16 = jnp.bfloat16
F32 = jnp.float32
HD = 128
GROUP = 12
TOK = 64
PRE = 256
HALF = PRE // 2
ROWS = GROUP * TOK
N_CTX = 16
N_TP = 8
CACHE = 2048
CBLK = 128
DOUT = 768
LOG2E = 1.4426950408889634
SCALE2 = HD**-0.5 * LOG2E
CHUNK = 256
NEG = -1e30
NT = (((1,), (1,)), ((), ()))


def column(row):
    n = row.shape[1]
    wide = jnp.broadcast_to(row.astype(F32), (n, n))
    on = lax.broadcasted_iota(jnp.int32, (n, n), 0) == lax.broadcasted_iota(jnp.int32, (n, n), 1)
    return jnp.sum(jnp.where(on, wide, 0.0), axis=1, keepdims=True)


def kernel(
    q_hbm, prefix, new, nexp, shift_in, dq, cache, cexp, clen_in, dnew, w, resid,
    out_attn, out_ship, out_dec,
    gp, gn, ne, q_in, q_rows, m_ref, acc_ref,
    dq_in, dq_rows, cache_v, ce, dn, ga, gb, gaf, w_v, t_out, t_in, res_v, ship_out, ship_in,
    part_o, part_s, back_o, back_s, far_v, shift, clen,
    lsem, ring_s, ring_r, q_s, q_r, at_s, at_r, tp_s, tp_r, sh_s, sh_r, po_s, po_r, ps_s, ps_r, far_s, far_r, near, z_sem,
):
    role, p, tp = lax.axis_index("role"), lax.axis_index("ctx"), lax.axis_index("tp")
    core = lax.rem(p, 2)
    z = p // 2
    right, left = lax.rem(p + 2, N_CTX), lax.rem(p + N_CTX - 2, N_CTX)
    sib = p + 1 - 2 * core

    y, x = lax.rem(tp, 4), 2 * role + tp // 4
    beside = [
        (x < 3, {"role": (x + 1) // 2, "tp": lax.rem(x + 1, 2) * 4 + y}),
        (x > 0, {"role": (x - 1) // 2, "tp": lax.rem(x + 3, 2) * 4 + y}),
        (y < 3, {"tp": tp + 1}),
        (y > 0, {"tp": tp - 1}),
    ]
    count = sum(there.astype(jnp.int32) for there, _ in beside)

    def tell(sem):
        for there, d in beside:

            @pl.when(there)
            def _(d=d):
                pl.semaphore_signal(sem, inc=1, device_id=d, device_id_type=MESH)

    bar = pltpu.get_barrier_semaphore()
    for d in ({"ctx": right}, {"ctx": left}, {"ctx": sib}):
        pl.semaphore_signal(bar, inc=1, device_id=d, device_id_type=MESH)
    tell(bar)

    loads = [
        (new.at[0], gn.at[z]), (nexp.at[0], ne), (prefix.at[0], gp.at[z]),
        (dq.at[0], dq_in), (cexp.at[0], ce), (dnew.at[0], dn),
        (cache.at[0, 0], cache_v.at[0]), (cache.at[0, 1], cache_v.at[1]),
        (q_hbm.at[0], q_in), (w, w_v), (resid.at[0], res_v), (shift_in, shift), (clen_in, clen),
    ]
    ld = [pltpu.make_async_copy(s, d, lsem.at[i]) for i, (s, d) in enumerate(loads)]
    pl.semaphore_wait(bar, 3 + count)

    dev = (right, left)
    kinds = {h: ((0, 1, 2), (0, 2, 1)) for h in (1, 2, 3)}
    kinds[4] = ((3, 1), (4, 2))
    slot = {}
    for dr in (0, 1):
        for h in (1, 2, 3, 4):
            for kd in kinds[h][dr]:
                slot[(dr, h, kd)] = len(slot)

    def part(src, kd):
        if kd == 0:
            return gn.at[src]
        if kd == 1:
            return gp.at[src, :, 0:HALF]
        if kd == 2:
            return gp.at[src, :, HALF:PRE]
        if kd == 3:
            return gn.at[src, 0]
        return gn.at[src, 1]

    def origin(dr, h):
        return lax.rem(z + (8 - h if dr == 0 else h), 8)

    def ring_copy(src, kd, dr, h, held=None):
        i = slot[(dr, h, kd)]
        return pltpu.make_async_remote_copy(
            src_ref=part(src, kd) if held is None else held, dst_ref=part(src, kd), send_sem=ring_s.at[i], recv_sem=ring_r.at[i],
            device_id={"ctx": dev[dr]}, device_id_type=MESH,
        )

    sends = []
    done = [0]

    def drain(upto):
        for c in sends[done[0] : upto]:
            c.wait_send()
        done[0] = max(done[0], upto)

    def start(c):
        c.start()
        sends.append(c)

    def post(j):
        for dr in (0, 1):
            kd = kinds[1][dr][j]
            src = new.at[0] if j == 0 else prefix.at[0, :, 0:HALF] if kd == 1 else prefix.at[0, :, HALF:PRE]
            start(ring_copy(z, kd, dr, 1, src))

    def pump(h, j):
        for dr in (0, 1):
            kd = kinds[h][dr][j]
            src = origin(dr, h)
            ring_copy(src, kd, dr, h).wait_recv()
            if h < 3:
                start(ring_copy(src, kd, dr, h + 1))
            elif h == 3:
                if kd == 0:
                    start(ring_copy(src, 3 + dr, dr, 4))
                elif kd == 1 + dr:
                    start(ring_copy(src, kd, dr, 4))

    def to_sib(src, dst, s, r):
        return pltpu.make_async_remote_copy(
            src_ref=src, dst_ref=dst, send_sem=s, recv_sem=r, device_id={"ctx": sib}, device_id_type=MESH
        )

    def decode(r):
        qr = dq_rows[16 * r : 16 * r + 16].astype(BF16)
        s = lax.dot_general(qr, cache_v[0, r], NT, preferred_element_type=F32)
        ek = jnp.exp2(column(ce[0, r])) * SCALE2
        ev = jnp.exp2(column(ce[1, r]))
        length = clen[0, r]
        lane = lax.broadcasted_iota(jnp.int32, (16, CBLK), 1)
        cols = []
        for b in range(CACHE // CBLK):
            x = s[:, b * CBLK : (b + 1) * CBLK] * ek[b : b + 1, :]
            cols.append(jnp.where(lane < length - b * CBLK, x, NEG))
        kn = dn[0, r : r + 1].astype(F32)
        vn = dn[1, r : r + 1].astype(F32)
        own = jnp.sum(qr.astype(F32) * kn, axis=1, keepdims=True) * SCALE2
        top = cols[0]
        for x in cols[1:]:
            top = jnp.maximum(top, x)
        top = jnp.maximum(jnp.max(top, axis=1, keepdims=True), own)
        tot = jnp.zeros((16, CBLK), F32)
        pv = []
        for b, x in enumerate(cols):
            e = jnp.exp2(x - top)
            tot = tot + e
            pv.append((e * ev[b : b + 1, :]).astype(BF16))
        own = jnp.exp2(own - top)
        total = jnp.sum(tot, axis=1, keepdims=True) + own
        o = jnp.dot(jnp.concatenate(pv, axis=1), cache_v[1, r], preferred_element_type=F32)
        o = o + own.astype(BF16).astype(F32) * vn
        fac = jnp.concatenate([jnp.zeros((12, 1), F32), jnp.exp2(-column(ne[r]))], axis=0)
        row = lax.broadcasted_iota(jnp.int32, (16, HD), 0)
        ga[z, 16 * r : 16 * r + 16] = jnp.where(row < GROUP, o / total, fac).astype(BF16)

    def attend(blocks, half, first=False, fresh=False, each=None):
        if fresh:
            blocks = blocks + [(gn.at[i, 0], gn.at[i, 1]) for i in range(8)]
        keys = jnp.concatenate([b[0][...] for b in blocks], axis=0)
        n = keys.shape[0]
        vals = jnp.concatenate([b[1][...] for b in blocks], axis=0)
        vals = jnp.concatenate([vals, jnp.ones((n, HD), BF16)], axis=1)
        chunks = [pl.ds(half * ROWS + c * CHUNK, CHUNK) for c in range(ROWS // CHUNK)]

        def scores(c):
            s = lax.dot_general(q_rows[chunks[c]], keys, NT, preferred_element_type=F32)
            return [s[:, j : j + HD] for j in range(0, n, HD)]

        s = scores(0)
        for c, rows in enumerate(chunks):
            later = scores(c + 1) if c + 1 < len(chunks) else None
            if fresh:
                lane = lax.broadcasted_iota(jnp.int32, (CHUNK, HD), 1)
                key = (lane // TOK) * (2 * TOK) + lax.rem(lane, TOK) + core * TOK
                tok = lax.rem(lax.broadcasted_iota(jnp.int32, (CHUNK, HD), 0), TOK) + (sib if half else p) * TOK
                for j in range(4):
                    i = len(s) - 4 + j
                    s[i] = jnp.where(key + j * (4 * TOK) <= tok, s[i], NEG)
            top = s[0]
            for x in s[1:]:
                top = jnp.maximum(top, x)
            top = jnp.broadcast_to(jnp.max(top, axis=1, keepdims=True), (CHUNK, HD))
            if not first:
                before = m_ref[rows]
                top = jnp.maximum(before, top)
            e = jnp.concatenate([jnp.exp2((x - top) * SCALE2).astype(BF16) for x in s], axis=1)
            o = jnp.dot(e, vals, preferred_element_type=F32)
            if not first:
                keep = jnp.exp2((before - top) * SCALE2)
                o = o + acc_ref[rows] * jnp.concatenate([keep, keep], axis=1)
            if each is not None:
                each(c, o, top)
            else:
                acc_ref[rows] = o
                m_ref[rows] = top
            s = later

    def pref(src):
        return (gp.at[src, 0], gp.at[src, 1])

    post(0)
    post(1)
    post(2)
    along = [{"ctx": right}, {"ctx": left}]
    for d in along:
        pl.semaphore_signal(z_sem.at[0], inc=1, device_id=d, device_id_type=MESH)
    for i in (8, 3, 1, 4, 5, 12, 6, 7, 2, 0, 9, 10, 11):
        ld[i].start()
    tell(near.at[0])
    part_s[...] = jnp.zeros(part_s.shape, F32)
    ld[8].wait()
    for h in range(GROUP):
        q_rows[h * TOK : (h + 1) * TOK, :] = q_in[:, h * HD : (h + 1) * HD]
    q_copy = to_sib(q_rows.at[0:ROWS], q_rows.at[ROWS : 2 * ROWS], q_s.at[0], q_r.at[0])
    start(q_copy)
    ld[3].wait()
    x = dq_in[...].astype(F32)
    dq_rows[...] = jnp.zeros((32, HD), F32)
    for r in range(2):
        for h in range(GROUP):
            dq_rows[16 * r + h : 16 * r + h + 1, :] = x[r : r + 1, h * HD : (h + 1) * HD]
    for i in (1, 4, 5, 6, 7, 12):
        ld[i].wait()
    decode(0)
    decode(1)

    def at_send(*steps):
        for d in steps:
            c = pltpu.make_async_remote_copy(
                src_ref=ga.at[z], dst_ref=ga.at[z], send_sem=at_s.at[d], recv_sem=at_r.at[d],
                device_id={"ctx": lax.rem(p + 2 * d, N_CTX)}, device_id_type=MESH,
            )
            start(c)

    def next_z(i, more):
        pl.semaphore_wait(z_sem.at[i], 2)
        if i < 2:
            for d in along:
                pl.semaphore_signal(z_sem.at[i + 1], inc=1, device_id=d, device_id_type=MESH)
        at_send(*more)

    next_z(0, (1, 7, 2, 6))
    pump(1, 0)
    next_z(1, (3, 5))
    pl.semaphore_wait(near.at[0], count)
    tell(near.at[1])
    pump(1, 1)
    pump(1, 2)
    next_z(2, (4,))
    pl.semaphore_wait(near.at[1], count)
    tell(near.at[2])
    one = [pref(z), pref(origin(0, 1)), pref(origin(1, 1))]
    ld[2].wait()
    attend(one, 0, first=True)
    pump(2, 0)
    q_copy.wait_recv()
    attend(one, 1, first=True)
    old = len(sends)
    pump(2, 1)
    pump(2, 2)
    pump(3, 0)
    two = [pref(origin(0, 2)), pref(origin(1, 2))]
    attend(two, 0)
    for d in range(1, 8):
        zs = lax.rem(z + 8 - d, 8)
        to_sib(ga.at[zs], ga.at[zs], at_s.at[d], at_r.at[d]).wait_recv()
    start(to_sib(ga, gb, at_s.at[0], at_r.at[0]))
    drain(old)
    old = len(sends)
    attend(two, 1)
    pump(3, 1)
    pump(3, 2)
    pump(4, 0)
    ld[0].wait()
    ships = []
    ld[11].wait()
    for o, owner in enumerate((p, sib)):
        for j in range(4):
            src = lax.rem(owner + N_CTX - shift[role, j], N_CTX)
            mine = lax.rem(src, 2) == core
            for k in range(2):
                f = ga[src // 2, 16 * k : 16 * k + 16].astype(F32)
                raw = gn[src // 2, k, 16 * j : 16 * j + 16].astype(F32)
                code = raw * f[GROUP + j : GROUP + j + 1, :]
                ship_out[o, k, 16 * j : 16 * j + 16] = jnp.where(mine, code, 0.0).astype(BF16)
        c = pltpu.make_async_remote_copy(
            src_ref=ship_out.at[o], dst_ref=ship_in.at[o], send_sem=sh_s.at[o], recv_sem=sh_r.at[o],
            device_id={"role": 1 - role, "ctx": owner}, device_id_type=MESH,
        )
        start(c)
        ships.append(c)
    pl.semaphore_wait(near.at[2], count)
    to_sib(ga, gb, at_s.at[0], at_r.at[0]).wait_recv()
    ld[9].wait()
    for zz in range(8):
        gaf[pl.ds(pl.multiple_of((2 * zz + core) * 32, 32), 32), :] = ga[zz].astype(F32)
        gaf[pl.ds(pl.multiple_of((2 * zz + 1 - core) * 32, 32), 32), :] = gb[zz].astype(F32)
    a = jnp.concatenate([gaf[pl.ds(h, 32, stride=16), :] for h in range(GROUP)], axis=1).astype(BF16)
    terms = jnp.dot(a, w_v[...], preferred_element_type=F32)
    for t in range(N_TP):
        t_out[t, 0:4, :] = terms[4 * t : 4 * t + 4, 0 : DOUT // 2]
        t_out[t, 4:8, :] = terms[4 * t : 4 * t + 4, DOUT // 2 : DOUT]
    for d in range(1, N_TP):
        to = lax.rem(tp + d, N_TP)
        c = pltpu.make_async_remote_copy(
            src_ref=t_out.at[to], dst_ref=t_in.at[tp], send_sem=tp_s.at[d], recv_sem=tp_r.at[d],
            device_id={"tp": to}, device_id_type=MESH,
        )
        start(c)
    eye = lax.broadcasted_iota(jnp.int32, (HD, HD), 0) == lax.broadcasted_iota(jnp.int32, (HD, HD), 1)
    backs = []

    def give(c, o, top):
        part_o[c] = (o[:, 0:HD] / o[:, HD:]).astype(BF16)
        lse = top * SCALE2 + jnp.log2(o[:, HD:])
        for b in range(CHUNK // HD):
            x = jnp.where(eye, lse[b * HD : (b + 1) * HD], 0.0)
            part_s[c, b : b + 1, :] = jnp.sum(x, axis=0, keepdims=True)
        c1 = to_sib(part_o.at[c], back_o.at[c], po_s.at[c], po_r.at[c])
        c2 = to_sib(part_s.at[c], back_s.at[c], ps_s.at[c], ps_r.at[c])
        start(c1)
        start(c2)
        backs.append((c1, c2))

    def merge(c, o, top):
        mine = o[:, 0:HD] / o[:, HD:]
        lse = top * SCALE2 + jnp.log2(o[:, HD:])
        other = []
        for b in range(CHUNK // HD):
            x = jnp.where(eye, jnp.broadcast_to(back_s[c, b : b + 1, :], (HD, HD)), 0.0)
            other.append(jnp.broadcast_to(jnp.sum(x, axis=1, keepdims=True), (HD, HD)))
        other = jnp.concatenate(other, axis=0)
        peak = jnp.maximum(lse, other)
        wa = jnp.exp2(lse - peak)
        wb = jnp.exp2(other - peak)
        res = ((mine * wa + back_o[c].astype(F32) * wb) / (wa + wb)).astype(BF16)
        for b in range(CHUNK // TOK):
            h = c * (CHUNK // TOK) + b
            out_attn[0, :, h * HD : (h + 1) * HD] = res[b * TOK : (b + 1) * TOK]

    three = [pref(origin(0, 3)), pref(origin(1, 3))]
    attend(three, 1, fresh=True, each=give)
    attend(three, 0, fresh=True)
    drain(old)

    pump(4, 1)
    far = origin(0, 4)
    fars = []
    for i in (0, 1):
        c = to_sib(gp.at[far, :, i * HALF : (i + 1) * HALF], far_v.at[:, i * HALF : (i + 1) * HALF], far_s.at[i], far_r.at[i])
        start(c)
        fars.append(c)
    for x in backs:
        for c in x:
            c.wait_recv()
    for c in fars:
        c.wait_recv()
    attend([pref(far), (far_v.at[0], far_v.at[1])], 0, each=merge)
    total = t_out[tp]
    for d in range(1, N_TP):
        frm = lax.rem(tp + N_TP - d, N_TP)
        pltpu.make_async_remote_copy(
            src_ref=t_out.at[frm], dst_ref=t_in.at[frm], send_sem=tp_s.at[d], recv_sem=tp_r.at[d],
            device_id={"tp": frm}, device_id_type=MESH,
        ).wait_recv()
        total = total + t_in[frm]
    ld[10].wait()
    wide = jnp.concatenate([total[0:4], total[4:8]], axis=1)
    out_dec[0] = (res_v[...].astype(F32) + wide).astype(BF16)

    for c in ships:
        c.wait_recv()
    out_ship[0] = (ship_in[0].astype(F32) + ship_in[1].astype(F32)).astype(BF16)
    drain(len(sends))


def hand_out(*refs):
    srcs, dsts, sem = refs[:3], refs[3:6], refs[6]
    cs = [pltpu.make_async_copy(a, b, sem.at[i]) for i, (a, b) in enumerate(zip(srcs, dsts))]
    for c in cs:
        c.start()
    for c in cs:
        c.wait()


def per_device(*args):
    args = list(args)
    args[3] = jnp.swapaxes(args[3], -1, -2)
    args[7] = jnp.swapaxes(args[7], -1, -2)
    out = main(*args)
    return pl.pallas_call(
        hand_out,
        out_shape=tuple(pltpu.HBM(x.shape, x.dtype) for x in out),
        in_specs=[pl.BlockSpec(memory_space=pltpu.VMEM)] * 3,
        out_specs=(pl.BlockSpec(memory_space=pltpu.HBM),) * 3,
        scratch_shapes=[pltpu.SemaphoreType.DMA((3,))],
    )(*[pltpu.with_memory_space_constraint(x, pltpu.VMEM) for x in out])


def main(*args):
    hb = pl.BlockSpec(memory_space=pltpu.HBM)
    dma = pltpu.SemaphoreType.DMA
    args = [pltpu.with_memory_space_constraint(a, pltpu.HBM) for a in args]
    return pl.pallas_call(
        kernel,
        out_shape=(
            pltpu.VMEM((1, TOK, GROUP * HD), BF16),
            pltpu.VMEM((1, 2, TOK, HD), BF16),
            pltpu.VMEM((1, 4, DOUT), BF16),
        ),
        in_specs=[hb] * len(args),
        out_specs=(pl.BlockSpec(memory_space=pltpu.VMEM),) * 3,
        scratch_shapes=[
            pltpu.VMEM((8, 2, PRE, HD), BF16),
            pltpu.VMEM((8, 2, TOK, HD), BF16),
            pltpu.VMEM((2, 1, 4), jnp.int32),
            pltpu.VMEM((TOK, GROUP * HD), BF16),
            pltpu.VMEM((2 * ROWS, HD), BF16),
            pltpu.VMEM((2 * ROWS, HD), F32),
            pltpu.VMEM((2 * ROWS, 2 * HD), F32),
            pltpu.VMEM((2, GROUP * HD), BF16),
            pltpu.VMEM((32, HD), F32),
            pltpu.VMEM((2, 2, CACHE, HD), BF16),
            pltpu.VMEM((2, 2, 1, CACHE // CBLK), jnp.int32),
            pltpu.VMEM((2, 2, HD), BF16),
            pltpu.VMEM((8, 32, HD), BF16),
            pltpu.VMEM((8, 32, HD), BF16),
            pltpu.VMEM((512, HD), F32),
            pltpu.VMEM((GROUP * HD, DOUT), BF16),
            pltpu.VMEM((N_TP, 8, DOUT // 2), F32),
            pltpu.VMEM((N_TP, 8, DOUT // 2), F32),
            pltpu.VMEM((4, DOUT), BF16),
            pltpu.VMEM((2, 2, TOK, HD), BF16),
            pltpu.VMEM((2, 2, TOK, HD), BF16),
            pltpu.VMEM((ROWS // CHUNK, CHUNK, HD), BF16),
            pltpu.VMEM((ROWS // CHUNK, 8, HD), F32),
            pltpu.VMEM((ROWS // CHUNK, CHUNK, HD), BF16),
            pltpu.VMEM((ROWS // CHUNK, 8, HD), F32),
            pltpu.VMEM((2, PRE, HD), BF16),
            pltpu.SMEM((2, 4), jnp.int32),
            pltpu.SMEM((1, 2), jnp.int32),
            dma((13,)),
            dma((22,)), dma((22,)),
            dma((1,)), dma((1,)),
            dma((8,)), dma((8,)),
            dma((8,)), dma((8,)),
            dma((2,)), dma((2,)),
            dma((3,)), dma((3,)),
            dma((3,)), dma((3,)),
            dma((2,)), dma((2,)),
            pltpu.SemaphoreType.REGULAR((3,)),
            pltpu.SemaphoreType.REGULAR((3,)),
        ],
        compiler_params=pltpu.CompilerParams(
            collective_id=0, has_side_effects=True, vmem_limit_bytes=48 * 2**20
        ),
    )(*args)


def solution(mesh):
    placed = (
        P("role", "ctx", "tp"),
        P("role", None, "ctx", "tp"),
        P("role", None, "ctx", "tp"),
        P("role", None, "ctx", "tp"),
        P(),
        P("role", "ctx", "tp"),
        P("role", None, "ctx", None, "tp"),
        P("role", None, "ctx", None, "tp"),
        P("role", "ctx"),
        P("role", None, "ctx", "tp"),
        P("tp", "ctx"),
        P("role", "tp", "ctx"),
    )
    return jax.shard_map(
        per_device,
        mesh=mesh,
        in_specs=placed,
        out_specs=(P("role", "ctx", "tp"), P("role", None, "ctx", "tp"), P("role", "tp", "ctx")),
        check_vma=False,
    )
```
